32 devices in a mesh: gx: 8 (over y, x, core), gy: 4 (over z).
Axes of the slice: x: 2, y: 2, z: 4, core: 2. Of those that a mesh axis runs over, the one named last changes fastest.
Arguments:
- coords: float32 [3, 8, 4, 128], P(None, 'gx', 'gy'), may hold values from 0 to 5
- atom_types: int32 [8, 4, 128], P('gx', 'gy'), may hold values 0 or 1
- neighbours: int32 [8, 4, 128, 128], P('gx', 'gy'), may hold values from 0 to 383
- send_x: int32 [8, 4, 2, 64], P('gx', 'gy'), may hold values from 0 to 127
- send_y: int32 [8, 4, 2, 64], P('gx', 'gy'), may hold values from 0 to 255
- poly_table: float32 [2, 6, 64], replicated, may hold values from -4 to 4
- fit_in: float32 [512, 128], replicated, may hold values from -0.25 to 0.25
- fit_hidden: float32 [2, 128, 128], replicated, may hold values from -0.5 to 0.5
- fit_bias: float32 [3, 128], replicated, may hold values from -3 to 3
- fit_out: float32 [128], replicated, may hold values from -0.5 to 0.5
- spectrum: float32 [2], replicated, may hold values from -0.02 to 0.1, as said below
- cheb_prev: float32 [4, 3, 8, 4, 128], P(None, None, 'gx', 'gy'), may hold values from -540 to 540
- cheb_cur: float32 [4, 3, 8, 4, 128], P(None, None, 'gx', 'gy'), may hold values from -540 to 540
Outputs:
- forces: float32 [3, 8, 4, 128], P(None, 'gx', 'gy')
- cheb_next: float32 [4, 3, 8, 4, 128], P(None, None, 'gx', 'gy')
- moments: float32 [2, 4], replicated
The draws below stay inside these ranges and needn't reach their ends.
Inputs may be any that keep to these rules, and one draw needn't show every extreme that they name: spectrum[0] lies in [-0.02, -0.01] and spectrum[1] in [0.05, 0.1].
All inputs are finite; a program needn't handle non-finite values. No bound on the sum of `atom_types` on one device may be relied on, other than what follows from the above.
Results may differ from the reference program's by a relative error of at most 0.00029.
Values sent between devices are 32-bit elements; how exact they have to be, the bound alone decides.
No kernel may reach another device: no remote copies, remote signals or barrier semaphores. Data moves between devices by JAX's collectives and lax.ppermute only.
A program may use at most 64 MiB of HBM per device.

```python
import math
import jax
import jax.numpy as jnp
from jax import lax

OWNED_ATOM_COUNT = 128
NEIGHBOUR_SLOTS = 128
M1 = 64
M2 = 8
FIT = 128
POLY = 6
ATOM_BLOCK = 32
GX = 64
GY = 64
GHOSTED_ATOMS = 384
BRICKS_ALONG_X = 8
BRICKS_ALONG_Y = 4


def vector_rule(key):
    base_key, spread_key = jax.random.split(key)
    shape = (4, 3, BRICKS_ALONG_X, BRICKS_ALONG_Y, OWNED_ATOM_COUNT)
    position = jnp.arange(BRICKS_ALONG_X).astype(jnp.float32) / max(BRICKS_ALONG_X - 1, 1)
    base = jnp.clip(jax.random.normal(base_key, shape, jnp.float32), -6.0, 6.0)
    ramp = 1.0 + 2.0 * position
    spread = jnp.exp(jax.random.uniform(spread_key, (1, 1, BRICKS_ALONG_X, BRICKS_ALONG_Y, OWNED_ATOM_COUNT), jnp.float32, 0.0, math.log(10.0)))
    return base * spread * ramp[None, None, :, None, None]


def draw_cheb_prev(key, part):
    return vector_rule(jax.random.fold_in(key, 11))


def draw_cheb_cur(key, part):
    return vector_rule(jax.random.fold_in(key, 23))


def draw_spectrum(key, part):
    lower_key, upper_key = jax.random.split(jax.random.fold_in(key, 37))
    lower = -jax.random.uniform(lower_key, (), jnp.float32, 0.01, 0.02)
    upper = jax.random.uniform(upper_key, (), jnp.float32, 0.05, 0.1)
    return jnp.stack([lower, upper])


def touch_ends(values, own_key, low, high):
    shape = values.shape
    place = [jax.random.randint(jax.random.fold_in(own_key, axis), (), 0, shape[axis]) for axis in range(len(shape))]
    values = values.at[tuple(place)].set(low)
    longest = shape.index(max(shape))
    place[longest] = (place[longest] + 1) % shape[longest]
    return values.at[tuple(place)].set(high)


def level_of(rng, dims, pieces, low, largest):
    loudness = 1.0
    for dim, parts in pieces:
        draws = jax.random.uniform(jax.random.fold_in(jax.random.fold_in(rng, 6), dim), (parts,), jnp.float32, low / len(pieces), largest / len(pieces))
        loudness = loudness * jnp.repeat(jnp.exp(draws), dims[dim] // parts).reshape((-1,) + (1,) * (len(dims) - 1 - dim))
    return loudness


def normal_values(key, dims, scale, most, held_as=jnp.bfloat16):
    return jnp.clip(scale * jax.random.normal(key, dims, jnp.float32), -most, most).astype(held_as)


def setup_inputs(seed: int = 0) -> dict:
    key_of = jax.random.split(jax.random.key(seed), 14)
    coords = jnp.clip(5.0 * jax.random.uniform(key_of[0], (3, BRICKS_ALONG_X, BRICKS_ALONG_Y, OWNED_ATOM_COUNT), jnp.float32) ** level_of(key_of[0], (3, BRICKS_ALONG_X, BRICKS_ALONG_Y, OWNED_ATOM_COUNT), ((1, 8), (2, 4)), -0.2, 0.2), 0.0, 5.0)
    atom_types = touch_ends((jax.random.randint(key_of[1], (BRICKS_ALONG_X, BRICKS_ALONG_Y, OWNED_ATOM_COUNT), 0, 8) < 1).astype(jnp.int32), jax.random.fold_in(key_of[1], 1), 0, 1)
    neighbours = touch_ends(jax.random.randint(key_of[2], (BRICKS_ALONG_X, BRICKS_ALONG_Y, OWNED_ATOM_COUNT, NEIGHBOUR_SLOTS), 0, GHOSTED_ATOMS), jax.random.fold_in(key_of[2], 1), 0, GHOSTED_ATOMS - 1).astype(jnp.int32)
    send_x = touch_ends(jax.random.randint(key_of[3], (BRICKS_ALONG_X, BRICKS_ALONG_Y, 2, GX), 0, OWNED_ATOM_COUNT), jax.random.fold_in(key_of[3], 1), 0, OWNED_ATOM_COUNT - 1).astype(jnp.int32)
    send_y = touch_ends(jax.random.randint(key_of[4], (BRICKS_ALONG_X, BRICKS_ALONG_Y, 2, GY), 0, OWNED_ATOM_COUNT + 2 * GX), jax.random.fold_in(key_of[4], 1), 0, (OWNED_ATOM_COUNT + 2 * GX) - 1).astype(jnp.int32)
    poly_table = normal_values(key_of[5], (2, POLY, M1), 1.0, 4.0, jnp.float32)
    fit_in = normal_values(key_of[6], (M1 * M2, FIT), (M1 * M2) ** -0.5, 0.25, jnp.float32)
    fit_hidden = normal_values(key_of[7], (2, FIT, FIT), FIT ** -0.5, 0.5, jnp.float32)
    fit_bias = normal_values(key_of[8], (3, FIT), 0.5, 3.0, jnp.float32)
    fit_out = normal_values(key_of[9], (FIT,), FIT ** -0.5, 0.5, jnp.float32)
    spectrum = draw_spectrum(jax.random.fold_in(key_of[13], 71), 0)
    cheb_prev = draw_cheb_prev(jax.random.fold_in(key_of[13], 71), 0)
    cheb_cur = draw_cheb_cur(jax.random.fold_in(key_of[13], 71), 0)
    return dict(coords=coords, atom_types=atom_types, neighbours=neighbours, send_x=send_x, send_y=send_y, poly_table=poly_table, fit_in=fit_in, fit_hidden=fit_hidden, fit_bias=fit_bias, fit_out=fit_out, spectrum=spectrum, cheb_prev=cheb_prev, cheb_cur=cheb_cur)


BRICK = 5.0
SOFTENING = 0.25
CUTOFF_SQ = 16.0
HIGHEST = lax.Precision.HIGHEST

def site_energy(offsets, near_kind, poly_table, fit_in, fit_hidden, fit_bias, fit_out):
    radius_sq = lax.optimization_barrier(jnp.sum(offsets * offsets, axis=0))
    soft_radius = jnp.sqrt(radius_sq + SOFTENING)
    switch = 1.0 / (1.0 + radius_sq / CUTOFF_SQ)
    environ = jnp.concatenate([switch[None], switch[None] * offsets / soft_radius[None]], axis=0)
    powers = jnp.stack([switch ** degree for degree in range(poly_table.shape[1])], axis=0)
    silicon = jnp.einsum('kbs,km->mbs', powers, poly_table[0], precision=HIGHEST)
    hydrogen = jnp.einsum('kbs,km->mbs', powers, poly_table[1] - poly_table[0], precision=HIGHEST)
    embedded = silicon + near_kind[None] * hydrogen
    contracted = jnp.einsum('cbs,mbs->cmb', environ, embedded, precision=HIGHEST) / offsets.shape[2]
    descriptor = jnp.einsum('cmb,cnb->mnb', contracted, contracted[:, :M2], precision=HIGHEST)
    descriptor = descriptor.reshape(-1, offsets.shape[1])
    hidden_layer = jnp.tanh(jnp.dot(fit_in.T, descriptor, precision=HIGHEST) + fit_bias[0][:, None])
    hidden_layer = jnp.tanh(jnp.dot(fit_hidden[0].T, hidden_layer, precision=HIGHEST) + fit_bias[1][:, None]) + hidden_layer
    hidden_layer = jnp.tanh(jnp.dot(fit_hidden[1].T, hidden_layer, precision=HIGHEST) + fit_bias[2][:, None]) + hidden_layer
    return jnp.sum(jnp.dot(fit_out, hidden_layer, precision=HIGHEST))

def block_terms(ghosted, slot_rows, first_atom, params):
    block_atoms = slot_rows.shape[0]
    centre = lax.dynamic_slice_in_dim(ghosted, first_atom, block_atoms, 1)
    picked = jnp.take(ghosted, slot_rows.reshape(-1), axis=1).reshape(ghosted.shape[0], block_atoms, -1)
    offsets = picked[0:3] - centre[0:3, :, None]
    near_kind = picked[3]
    tangents = (picked[4:16] - centre[4:16, :, None]).reshape(4, 3, block_atoms, -1)

    def energy_of(moved):
        return site_energy(moved, near_kind, *params)
    gradient, linear = jax.vjp(jax.grad(energy_of), offsets)
    curvature = jax.vmap(lambda vector: linear(vector)[0])(tangents)
    return jnp.concatenate([gradient, curvature.reshape(12, block_atoms, -1)], axis=0)

def brick_sum(ghosted, near_lists, params):
    block_size = ATOM_BLOCK

    def advance(accumulated, number):
        first_atom = number * block_size
        slot_rows = lax.dynamic_slice_in_dim(near_lists, first_atom, block_size, 0)
        terms = block_terms(ghosted, slot_rows, first_atom, params)
        accumulated = accumulated.at[:, slot_rows.reshape(-1)].add(terms.reshape(15, -1))
        centre_sum = lax.dynamic_slice_in_dim(accumulated, first_atom, block_size, 1) - lax.optimization_barrier(jnp.sum(terms, axis=2))
        accumulated = lax.dynamic_update_slice_in_dim(accumulated, centre_sum, first_atom, 1)
        return (accumulated, None)
    start_sum = jnp.zeros((15, ghosted.shape[1]), jnp.float32)
    blocks = jnp.arange(near_lists.shape[0] // block_size, dtype=jnp.int32)
    accumulated, unused = lax.scan(advance, start_sum, blocks)
    return accumulated

def outgoing(field, lists):
    return jnp.stack([field[:, lists[0]], field[:, lists[1]]], axis=0)

def returned(accumulated, lists, lower_terms, upper_terms):
    return accumulated.at[:, lists[0]].add(lower_terms).at[:, lists[1]].add(upper_terms)

def reference(coords, atom_types, neighbours, send_x, send_y, poly_table, fit_in, fit_hidden, fit_bias, fit_out, spectrum, cheb_prev, cheb_cur):
    kind = atom_types.astype(jnp.float32)
    light = 1.008 ** (-0.5)
    heavy = 28.0855 ** (-0.5)
    scale = heavy + kind * (light - heavy)
    lent = cheb_cur * scale[None, None]
    field = jnp.concatenate([coords, kind[None], lent.reshape(12, BRICKS_ALONG_X, BRICKS_ALONG_Y, OWNED_ATOM_COUNT)], axis=0)
    field = jnp.transpose(field, (1, 2, 0, 3))
    sent = jax.vmap(jax.vmap(outgoing))(field, send_x)
    from_lower = jnp.roll(sent[:, :, 1], 1, axis=0).at[:, :, 0].add(-BRICK)
    from_upper = jnp.roll(sent[:, :, 0], -1, axis=0).at[:, :, 0].add(BRICK)
    first = jnp.concatenate([field, from_lower, from_upper], axis=3)
    sent = jax.vmap(jax.vmap(outgoing))(first, send_y)
    from_below = jnp.roll(sent[:, :, 1], 1, axis=1).at[:, :, 1].add(-BRICK)
    from_above = jnp.roll(sent[:, :, 0], -1, axis=1).at[:, :, 1].add(BRICK)
    ghosted = jnp.concatenate([first, from_below, from_above], axis=3)
    params = (poly_table, fit_in, fit_hidden, fit_bias, fit_out)
    flat_ghosted = ghosted.reshape(BRICKS_ALONG_X * BRICKS_ALONG_Y, 16, GHOSTED_ATOMS)
    flattened_lists = neighbours.reshape(BRICKS_ALONG_X * BRICKS_ALONG_Y, OWNED_ATOM_COUNT, NEIGHBOUR_SLOTS)
    accumulated = lax.map(lambda pair: brick_sum(pair[0], pair[1], params), (flat_ghosted, flattened_lists))
    accumulated = accumulated.reshape(BRICKS_ALONG_X, BRICKS_ALONG_Y, 15, GHOSTED_ATOMS)
    split = OWNED_ATOM_COUNT + 2 * GX
    lower_part = accumulated[..., split:split + GY]
    upper_part = accumulated[..., split + GY:]
    returned_y = jax.vmap(jax.vmap(returned))(accumulated[..., :split], send_y, jnp.roll(upper_part, 1, axis=1), jnp.roll(lower_part, -1, axis=1))
    lower_part = returned_y[..., OWNED_ATOM_COUNT:OWNED_ATOM_COUNT + GX]
    upper_part = returned_y[..., OWNED_ATOM_COUNT + GX:]
    own = jax.vmap(jax.vmap(returned))(returned_y[..., :OWNED_ATOM_COUNT], send_x, jnp.roll(upper_part, 1, axis=0), jnp.roll(lower_part, -1, axis=0))
    forces = -jnp.transpose(own[:, :, 0:3], (2, 0, 1, 3))
    curvature = jnp.transpose(own[:, :, 3:15].reshape(BRICKS_ALONG_X, BRICKS_ALONG_Y, 4, 3, OWNED_ATOM_COUNT), (2, 3, 0, 1, 4))
    center = (spectrum[0] + spectrum[1]) / 2.0
    half_width = (spectrum[1] - spectrum[0]) / 2.0
    cheb_next = 2.0 * (scale[None, None] * curvature - center * cheb_cur) / half_width - cheb_prev
    entries = 3.0 * OWNED_ATOM_COUNT * BRICKS_ALONG_X * BRICKS_ALONG_Y
    norm_part = lax.optimization_barrier(jnp.sum(cheb_cur * cheb_cur, axis=(1, 2, 3, 4))) / entries
    cross_part = lax.optimization_barrier(jnp.sum(cheb_next * cheb_cur, axis=(1, 2, 3, 4))) / entries
    return (forces, cheb_next, jnp.stack([norm_part, cross_part], axis=0))
```

```python
import functools

import jax
import jax.numpy as jnp
from jax import lax
from jax.experimental import pallas as pl
from jax.experimental.pallas import tpu as pltpu
from jax.sharding import PartitionSpec as P

BRICK = 5.0
SOFTENING = 0.25
CUTOFF_SQ = 16.0
LIGHT = 1.008 ** (-0.5)
HEAVY = 28.0855 ** (-0.5)
LANES = 128
SUBLANES = 8
M2 = 8
HALF = 64
F32 = jnp.float32
BF16 = jnp.bfloat16
VMEM = pl.BlockSpec(memory_space=pltpu.VMEM)
SMEM = pl.BlockSpec(memory_space=pltpu.SMEM)


def shape(*dims, dtype=F32):
    return jax.ShapeDtypeStruct(dims, dtype)


def call(body, outs, specs, scratch=(), flops=0, limit=None):
    return pl.pallas_call(
        body,
        out_shape=outs,
        in_specs=specs,
        out_specs=jax.tree.map(lambda _: VMEM, outs),
        scratch_shapes=list(scratch),
        compiler_params=pltpu.CompilerParams(vmem_limit_bytes=limit),
        cost_estimate=pl.CostEstimate(flops=flops, bytes_accessed=1 << 16, transcendentals=0),
    )


def halves(x):
    high = x.astype(BF16)
    return high, (x - high.astype(F32)).astype(BF16)


def dot(a, b, contract=((1,), (0,))):
    return lax.dot_general(a, b, (contract, ((), ())), preferred_element_type=F32)


def dot3(a, b, contract=((1,), (0,))):
    return dot(a[0], b[0], contract) + (dot(a[0], b[1], contract) + dot(a[1], b[0], contract))


def lane_take(row, index):
    return jnp.take_along_axis(
        jnp.broadcast_to(row, index.shape), index, axis=1, mode="promise_in_bounds"
    )


def lane_number(rows):
    return lax.broadcasted_iota(jnp.int32, (rows, LANES), 1)


def take_columns(parts, lists):
    low = jnp.broadcast_to(lists & (LANES - 1), (SUBLANES, LANES))
    chunk = jnp.broadcast_to(lists >> 7, (SUBLANES, LANES))
    rows = []
    for base in range(0, 16, SUBLANES):
        value = jnp.take_along_axis(
            parts[0][base : base + SUBLANES], low, axis=1, mode="promise_in_bounds"
        )
        for number in range(1, len(parts)):
            other = jnp.take_along_axis(
                parts[number][base : base + SUBLANES], low, axis=1, mode="promise_in_bounds"
            )
            value = jnp.where(chunk == number, other, value)
        rows.append(value)
    return jnp.concatenate(rows, axis=0)


def add_columns(values, lists, columns):
    high, low = halves(values)
    places = lax.broadcasted_iota(jnp.int32, (columns, LANES), 0)
    hot = (places == jnp.broadcast_to(lists, (columns, LANES))).astype(F32).astype(BF16)
    summed = dot(jnp.concatenate([high, low], axis=0), hot, ((1,), (1,)))
    return summed[0:16] + summed[16:32]


def joined(lower, upper, row):
    lanes = lane_number(16)
    rows = lax.broadcasted_iota(jnp.int32, (16, LANES), 0)
    shift = jnp.where(rows == row, jnp.where(lanes < HALF, -BRICK, BRICK), 0.0)
    return jnp.where(lanes < HALF, lower, upper) + shift


def params_body(
    poly_ref, fit_ref, hidden_ref, bias_ref, out_ref, nb_ref,
    ws_ref, wst_ref, hid_ref, hidt_ref, cols_ref, nbt_ref,
    table, mixed, square, columns,
):
    table[...] = jnp.zeros_like(table)
    table[0:6, :] = poly_ref[0]
    table[6:12, :] = poly_ref[1] - poly_ref[0]
    features = table[...]
    split_features = halves(features)
    for n in range(M2):
        picked = fit_ref[pl.ds(n, HALF, stride=M2), :]
        mixed[pl.ds(n, 16, stride=M2), :] = dot3(split_features, halves(picked))
    axis_features = halves(features[:, 0:M2])
    for k in range(16):
        block = mixed[k * M2 : (k + 1) * M2, :]
        square[k * 16 : (k + 1) * 16, :] = dot3(axis_features, halves(block))
    for k in range(12):
        block = square[k * 16 : (k + 1) * 16, :] + square[pl.ds(k, 16, stride=16), :]
        ws_ref[k * 16 : (k + 1) * 16, :] = 0.5 * block
    ws_ref[192:256, :] = jnp.zeros((64, LANES), F32)
    wst_ref[:, 0:128] = ws_ref[0:128, :].T
    wst_ref[:, 128:256] = ws_ref[128:256, :].T
    for layer in range(2):
        high, low = halves(hidden_ref[layer])
        hid_ref[layer, 0] = high
        hid_ref[layer, 1] = low
        high, low = halves(hidden_ref[layer].T)
        hidt_ref[layer, 0] = high
        hidt_ref[layer, 1] = low
    columns[...] = jnp.zeros_like(columns)
    columns[0:3, :] = bias_ref[...]
    columns[3:4, :] = out_ref[...].reshape(1, LANES)
    cols_ref[...] = columns[...].T
    nbt_ref[...] = nb_ref[0, 0].T


def field_body(coords_ref, types_ref, cur_ref, prev_ref, send_ref, field_ref, sent_ref, sums_ref):
    kind = types_ref[0].astype(F32)
    scale = HEAVY + kind * (LIGHT - HEAVY)
    for a in range(3):
        field_ref[a : a + 1, :] = coords_ref[a, 0]
    field_ref[3:4, :] = kind
    lanes = lane_number(1)
    norm = jnp.zeros((1, LANES), F32)
    past = jnp.zeros((1, LANES), F32)
    for w in range(4):
        own = jnp.zeros((1, LANES), F32)
        old = jnp.zeros((1, LANES), F32)
        for b in range(3):
            current = cur_ref[w, b, 0]
            own += current * current
            old += current * prev_ref[w, b, 0]
            row = 4 + 3 * w + b
            field_ref[row : row + 1, :] = current * scale
        norm = jnp.where(lanes == w, jnp.sum(own, axis=1, keepdims=True), norm)
        past = jnp.where(lanes == w, jnp.sum(old, axis=1, keepdims=True), past)
    sums_ref[0:1, :] = norm
    sums_ref[1:2, :] = past
    lists = jnp.concatenate([send_ref[0, 0, 1:2, :], send_ref[0, 0, 0:1, :]], axis=1)
    sent_ref[...] = take_columns([field_ref[...]], lists)


def first_body(field_ref, lower_ref, upper_ref, send_ref, ghost_ref, sent_ref):
    ghost = joined(lower_ref[...], upper_ref[...], 0)
    ghost_ref[...] = ghost
    lists = jnp.concatenate([send_ref[0, 0, 1:2, :], send_ref[0, 0, 0:1, :]], axis=1)
    sent_ref[...] = take_columns([field_ref[...], ghost], lists)


def pair_body(
    entries, slots,
    spectrum_ref, field_ref, ghost_ref, lower_ref, upper_ref, nbt_ref,
    ws_ref, wst_ref, hid_ref, hidt_ref, cols_ref, sums_ref,
    terms_ref, share_ref,
    chunks, pair, power, moment, gee, form, back, lam,
):
    groups = slots // SUBLANES
    chunks[0] = field_ref[...]
    chunks[1] = ghost_ref[...]
    chunks[2] = joined(lower_ref[...], upper_ref[...], 1)
    moment[...] = jnp.zeros_like(moment)

    def gather(group, carry):
        at = pl.ds(pl.multiple_of(group * SUBLANES, SUBLANES), SUBLANES)
        index = nbt_ref[at, :]
        low = index & (LANES - 1)
        chunk = index >> 7
        second = chunk == 1
        third = chunk == 2
        rows = []
        for r in range(16):
            value = jnp.where(second, lane_take(chunks[1, r : r + 1, :], low), lane_take(chunks[0, r : r + 1, :], low))
            value = jnp.where(third, lane_take(chunks[2, r : r + 1, :], low), value)
            if r != 3:
                value = value - chunks[0, r : r + 1, :]
            pair[r, at, :] = value
            if r < 3:
                rows.append(value)
        x, y, z = rows
        radius_sq = x * x + y * y + z * z
        inverse = lax.rsqrt(radius_sq + SOFTENING)
        switch = 1.0 / (1.0 + radius_sq / CUTOFF_SQ)
        pair[16, at, :] = inverse
        value = switch
        for k in range(6):
            power[k, at, :] = value
            value = value * switch
        return carry

    lax.fori_loop(0, groups, gather, 0)

    zero = jnp.zeros((SUBLANES, LANES), F32)

    def sum_moments(w, parts):
        def body(group, totals):
            at = pl.ds(pl.multiple_of(group * SUBLANES, SUBLANES), SUBLANES)
            totals = list(totals)
            powers = [power[k, at, :] for k in range(6)]
            near = pair[3, at, :]
            inverse = pair[16, at, :]
            if w:
                d = [pair[a, at, :] for a in range(3)]
                v = [pair[1 + 3 * w + a, at, :] for a in range(3)]
                along = d[0] * v[0] + d[1] * v[1] + d[2] * v[2]
                tau = powers[0] * along * (-2.0 / CUTOFF_SQ)
                fall = inverse * inverse * along
            for place, c in enumerate(parts):
                if w == 0:
                    weight = None if c == 0 else pair[c - 1, at, :] * inverse
                elif c == 0:
                    weight, step = zero, tau
                else:
                    unit = d[c - 1] * inverse
                    step = tau * unit
                    weight = v[c - 1] * inverse - unit * fall
                for k in range(6):
                    if w:
                        weight = step if (c == 0 and k == 0) else weight + step
                    term = powers[k] if weight is None else powers[k] * weight
                    totals[place * 12 + k] += term
                    totals[place * 12 + 6 + k] += near * term
            return tuple(totals)

        totals = lax.fori_loop(0, groups, body, (zero,) * (12 * len(parts)))
        for place, c in enumerate(parts):
            for k in range(12):
                row = ((w * 4 + c) * 16 + k) * SUBLANES
                moment[row : row + SUBLANES, :] = totals[place * 12 + k]

    for w in range(5):
        sum_moments(w, (0, 1))
        sum_moments(w, (2, 3))

    for block in range(20):
        total = moment[pl.ds(block * 128, 16, stride=SUBLANES), :]
        for sub in range(1, SUBLANES):
            total += moment[pl.ds(block * 128 + sub, 16, stride=SUBLANES), :]
        gee[block] = total * (1.0 / slots)

    for k in range(12):
        for w in range(5):
            total = gee[w * 4] * gee[0, k : k + 1, :]
            for c in range(1, 4):
                total += gee[w * 4 + c] * gee[c, k : k + 1, :]
            form[k * 16 : (k + 1) * 16, w * LANES : (w + 1) * LANES] = total * 2.0 if w == 0 else total * 4.0
    form[192:256, :] = jnp.zeros((64, 5 * LANES), F32)

    def wide(column):
        return jnp.broadcast_to(column, (LANES, LANES))

    def cut(x, w):
        return x[:, w * LANES : (w + 1) * LANES]

    def layer(pre, bias):
        bent = jnp.tanh(cut(pre, 0) + wide(bias))
        slope = 1.0 - bent * bent
        return bent, slope

    pre1 = dot3(halves(wst_ref[...] * 0.5), halves(form[...]))
    bent1, slope1 = layer(pre1, cols_ref[:, 0:1])
    hidden1 = [bent1] + [slope1 * cut(pre1, w) for w in range(1, 5)]
    pre2 = dot3((hidt_ref[0, 0], hidt_ref[0, 1]), halves(jnp.concatenate(hidden1, axis=1)))
    bent2, slope2 = layer(pre2, cols_ref[:, 1:2])
    hidden2 = [bent2 + hidden1[0]] + [slope2 * cut(pre2, w) + hidden1[w] for w in range(1, 5)]
    pre3 = dot3((hidt_ref[1, 0], hidt_ref[1, 1]), halves(jnp.concatenate(hidden2, axis=1)))
    bent3, slope3 = layer(pre3, cols_ref[:, 2:3])
    out = wide(cols_ref[:, 3:4])
    adj3 = [out * slope3] + [(-2.0 * out * bent3 * slope3) * cut(pre3, w) for w in range(1, 5)]
    up2 = dot3((hid_ref[1, 0], hid_ref[1, 1]), halves(jnp.concatenate(adj3, axis=1)))
    up2 = [cut(up2, 0) + out] + [cut(up2, w) for w in range(1, 5)]
    bend2 = -2.0 * up2[0] * bent2 * slope2
    adj2 = [up2[0] * slope2] + [up2[w] * slope2 + bend2 * cut(pre2, w) for w in range(1, 5)]
    up1 = dot3((hid_ref[0, 0], hid_ref[0, 1]), halves(jnp.concatenate(adj2, axis=1)))
    up1 = [cut(up1, w) + up2[w] for w in range(5)]
    bend1 = -2.0 * up1[0] * bent1 * slope1
    adj1 = [up1[0] * slope1] + [up1[w] * slope1 + bend1 * cut(pre1, w) for w in range(1, 5)]
    back[...] = dot3(halves(ws_ref[...]), halves(jnp.concatenate(adj1, axis=1)))

    for c in range(4):
        totals = [None] * 5
        for k in range(12):
            rows = slice(k * 16, (k + 1) * 16)
            base = back[rows, 0:LANES]
            plain = gee[c, k : k + 1, :]
            for w in range(5):
                if w == 0:
                    term = base * plain
                else:
                    term = back[rows, w * LANES : (w + 1) * LANES] * plain + base * gee[w * 4 + c, k : k + 1, :]
                totals[w] = term if k == 0 else totals[w] + term
        for w in range(5):
            lam[w * 4 + c] = totals[w] * (2.0 / slots)
            lam[w * 4 + c, 6:12, :] = lam[w * 4 + c, 0:6, :] + lam[w * 4 + c, 6:12, :]

    def push(group, quad):
        start = pl.multiple_of(group * SUBLANES, SUBLANES)
        at = pl.ds(start, SUBLANES)
        switch = power[0, at, :]
        inverse = pair[16, at, :]
        near = pair[3, at, :] > 0.5
        d = [pair[a, at, :] for a in range(3)]
        unit = [x * inverse for x in d]
        alpha = switch * (2.0 / CUTOFF_SQ)
        square = inverse * inverse
        quad = list(quad)

        def coefficients(w, c):
            return [
                jnp.where(near, lam[w * 4 + c, 6 + k : 7 + k, :], lam[w * 4 + c, k : k + 1, :])
                for k in range(6)
            ]

        def poly(values):
            total = values[5]
            for k in range(4, -1, -1):
                total = total * switch + values[k]
            return total * switch

        def store(row, value):
            terms_ref[pl.ds(start * 16 + row, SUBLANES, stride=16), :] = value

        plain, first, second = [], [], []
        for c in range(4):
            values = coefficients(0, c)
            plain.append(poly(values) if c else None)
            first.append(poly([values[k] * (k + 1.0) for k in range(6)]))
            second.append(poly([values[k] * ((k + 1.0) * (k + 1.0)) for k in range(6)]))

        def along(values):
            return values[1] * unit[0] + values[2] * unit[1] + values[3] * unit[2]

        plain_along = along(plain)
        first_along = along(first)
        first_sum = first[0] + first_along
        second_sum = second[0] + along(second)
        fall = -(alpha * first_sum + square * plain_along)
        for b in range(3):
            store(b, inverse * plain[b + 1] + d[b] * fall)
        bend = [-inverse * (square * plain[b + 1] + alpha * first[b + 1]) for b in range(3)]
        curl = (
            alpha * alpha * (first_sum + second_sum)
            + 2.0 * alpha * square * first_along
            + 3.0 * square * square * plain_along
        )
        for w in range(1, 5):
            values = [coefficients(w, c) for c in range(4)]
            p = [None] + [poly(values[c]) for c in range(1, 4)]
            f = [poly([values[c][k] * (k + 1.0) for k in range(6)]) for c in range(4)]
            down = -(alpha * (f[0] + along(f)) + square * along(p))
            v = [pair[1 + 3 * w + a, at, :] for a in range(3)]
            s = d[0] * v[0] + d[1] * v[1] + d[2] * v[2]
            t = s * curl + (bend[0] * v[0] + bend[1] * v[1] + bend[2] * v[2]) + down
            for b in range(3):
                term = bend[b] * s + v[b] * fall + d[b] * t + inverse * p[b + 1]
                store(3 * w + b, term)
                quad[w - 1] = quad[w - 1] + term * v[b]
        store(15, zero)
        return tuple(quad)

    quad = lax.fori_loop(0, groups, push, (zero,) * 4)

    lanes = lane_number(1)
    local = jnp.zeros((1, LANES), F32)
    for w in range(4):
        total = jnp.sum(jnp.sum(quad[w], axis=0, keepdims=True), axis=1, keepdims=True)
        local = jnp.where(lanes == w, total, local)
    center = (spectrum_ref[0] + spectrum_ref[1]) / 2.0
    width = (spectrum_ref[1] - spectrum_ref[0]) / 2.0
    norm = sums_ref[0:1, :]
    cross = 2.0 * (local - center * norm) / width - sums_ref[1:2, :]
    share = (norm + pltpu.roll(cross, 4, 1)) * (1.0 / entries)
    share_ref[...] = jnp.broadcast_to(share, share_ref.shape)


def scatter_body(slots, terms_ref, nbt_ref, accum_ref):
    per = SUBLANES
    places = lax.broadcasted_iota(jnp.int32, (LANES, LANES), 0)

    def body(group, carry):
        total, own = carry
        start = pl.multiple_of(group * per, per)
        lefts, rights = [], []
        for s in range(per):
            index = nbt_ref[pl.ds(start + s, 1), :]
            values = terms_ref[pl.ds((start + s) * 16, 16), :]
            own = own + values
            high, low = halves(values)
            chunk = index >> 7
            masks = [jnp.broadcast_to((chunk == c).astype(F32), (16, LANES)).astype(BF16) for c in range(3)]
            lefts.append(jnp.concatenate([x * m for m in masks for x in (high, low)], axis=0))
            hot = places == jnp.broadcast_to(index & (LANES - 1), (LANES, LANES))
            rights.append(hot.astype(F32).astype(BF16))
        left = jnp.concatenate(lefts, axis=1)
        right = jnp.concatenate(rights, axis=1)
        return total + dot(left, right, ((1,), (1,))), own

    total, own = lax.fori_loop(
        0, slots // per, body, (jnp.zeros((96, LANES), F32), jnp.zeros((16, LANES), F32))
    )
    for c in range(3):
        part = total[c * 32 : c * 32 + 16] + total[c * 32 + 16 : c * 32 + 32]
        accum_ref[c] = part - own if c == 0 else part


def fold_body(accum_ref, below_ref, above_ref, send_ref, own_ref, ghost_ref):
    lists = jnp.concatenate([send_ref[0, 0, 1:2, :], send_ref[0, 0, 0:1, :]], axis=1)
    values = jnp.where(lane_number(16) < HALF, above_ref[...], below_ref[...])
    added = add_columns(values, lists, 2 * LANES)
    own_ref[...] = accum_ref[0] + added[:, 0:LANES]
    ghost_ref[...] = accum_ref[1] + added[:, LANES:]


def last_body(
    spectrum_ref, own_ref, below_ref, above_ref, send_ref, types_ref, cur_ref, prev_ref, shares_ref,
    forces_ref, next_ref, moments_ref,
):
    lists = jnp.concatenate([send_ref[0, 0, 1:2, :], send_ref[0, 0, 0:1, :]], axis=1)
    values = jnp.where(lane_number(16) < HALF, above_ref[...], below_ref[...])
    own = own_ref[...] + add_columns(values, lists, LANES)
    scale = HEAVY + types_ref[0].astype(F32) * (LIGHT - HEAVY)
    center = (spectrum_ref[0] + spectrum_ref[1]) / 2.0
    width = (spectrum_ref[1] - spectrum_ref[0]) / 2.0
    for a in range(3):
        forces_ref[a, 0] = -own[a : a + 1]
    for w in range(4):
        for b in range(3):
            row = 3 + 3 * w + b
            current = cur_ref[w, b, 0]
            next_ref[w, b, 0] = (
                2.0 * (scale * own[row : row + 1] - center * current) / width - prev_ref[w, b, 0]
            )
    total = jnp.sum(shares_ref[...], axis=0, keepdims=True)
    moments_ref[0:1, :] = total[:, 0:4]
    moments_ref[1:2, :] = pltpu.roll(total, LANES - 4, 1)[:, 0:4]


def shifted(x, axis):
    devices = lax.axis_size(axis)
    up = [(i, (i + 1) % devices) for i in range(devices)]
    down = [(j, i) for i, j in up]
    return lax.ppermute(x, axis, up), lax.ppermute(x, axis, down)


def local(
    coords, atom_types, neighbours, send_x, send_y, poly_table, fit_in, fit_hidden, fit_bias,
    fit_out, spectrum, cheb_prev, cheb_cur,
):
    atoms, slots = neighbours.shape[2], neighbours.shape[3]
    devices = lax.axis_size("gx") * lax.axis_size("gy")
    entries = 3.0 * atoms * devices
    tile = shape(16, LANES)

    field, sent, sums = call(
        field_body, [tile, tile, shape(2, LANES)], [VMEM] * 5
    )(coords, atom_types, cheb_cur, cheb_prev, send_x)
    lower, upper = shifted(sent, "gx")
    ws, wst, hid, hidt, cols, nbt = call(
        params_body,
        [
            shape(256, LANES), shape(LANES, 256), shape(2, 2, 128, 128, dtype=BF16),
            shape(2, 2, 128, 128, dtype=BF16), shape(128, 128), shape(slots, atoms, dtype=jnp.int32),
        ],
        [VMEM] * 6,
        [pltpu.VMEM((16, HALF), F32), pltpu.VMEM((128, LANES), F32), pltpu.VMEM((256, LANES), F32), pltpu.VMEM((128, 128), F32)],
        flops=20_000_000,
    )(poly_table, fit_in, fit_hidden, fit_bias, fit_out, neighbours)
    ghost, sent = call(first_body, [tile, tile], [VMEM] * 4)(field, lower, upper, send_y)
    lower, upper = shifted(sent, "gy")
    terms, share = call(
        functools.partial(pair_body, entries, slots),
        [shape(slots * 16, LANES), shape(devices, LANES)],
        [SMEM] + [VMEM] * 11,
        [
            pltpu.VMEM((3, 16, LANES), F32),
            pltpu.VMEM((17, slots, LANES), F32),
            pltpu.VMEM((6, slots, LANES), F32),
            pltpu.VMEM((20 * 128, LANES), F32),
            pltpu.VMEM((20, 16, LANES), F32),
            pltpu.VMEM((256, 5 * LANES), F32),
            pltpu.VMEM((256, 5 * LANES), F32),
            pltpu.VMEM((20, 16, LANES), F32),
        ],
        flops=40_000_000,
        limit=32 << 20,
    )(spectrum, field, ghost, lower, upper, nbt, ws, wst, hid, hidt, cols, sums)
    shares = lax.all_to_all(share, ("gx", "gy"), 0, 0)
    accum = call(
        functools.partial(scatter_body, slots), shape(3, 16, LANES), [VMEM] * 2, flops=40_000_000
    )(terms, nbt)
    below, above = shifted(accum[2], "gy")
    own, ghost = call(fold_body, [tile, tile], [VMEM] * 4)(accum, below, above, send_y)
    below, above = shifted(ghost, "gx")
    return tuple(
        call(
            last_body,
            [shape(*coords.shape), shape(*cheb_cur.shape), shape(2, 4)],
            [SMEM] + [VMEM] * 8,
        )(spectrum, own, below, above, send_x, atom_types, cheb_cur, cheb_prev, shares)
    )


def solution(mesh):
    return jax.shard_map(
        local,
        mesh=mesh,
        in_specs=(
            P(None, "gx", "gy", None),
            P("gx", "gy", None),
            P("gx", "gy", None, None),
            P("gx", "gy", None, None),
            P("gx", "gy", None, None),
            P(),
            P(),
            P(),
            P(),
            P(),
            P(),
            P(None, None, "gx", "gy", None),
            P(None, None, "gx", "gy", None),
        ),
        out_specs=(P(None, "gx", "gy", None), P(None, None, "gx", "gy", None), P()),
        check_vma=False,
    )
```

```python
import functools

import jax
import jax.numpy as jnp
from jax import lax
from jax.experimental import pallas as pl
from jax.experimental.pallas import tpu as pltpu
from jax.sharding import PartitionSpec as P

BRICK = 5.0
SOFTENING = 0.25
CUTOFF_SQ = 16.0
LIGHT = 1.008 ** (-0.5)
HEAVY = 28.0855 ** (-0.5)
LANES = 128
SUBLANES = 8
M2 = 8
HALF = 64
F32 = jnp.float32
BF16 = jnp.bfloat16
VMEM = pl.BlockSpec(memory_space=pltpu.VMEM)


def shape(*dims, dtype=F32):
    return jax.ShapeDtypeStruct(dims, dtype)


def call(body, outs, specs, scratch=(), flops=0, limit=16 << 20):
    return pl.pallas_call(
        body,
        out_shape=outs,
        in_specs=specs,
        out_specs=jax.tree.map(lambda _: VMEM, outs),
        scratch_shapes=list(scratch),
        compiler_params=pltpu.CompilerParams(vmem_limit_bytes=limit),
        cost_estimate=pl.CostEstimate(flops=flops, bytes_accessed=1 << 16, transcendentals=0),
    )


def halves(x):
    high = x.astype(BF16)
    return high, (x - high.astype(F32)).astype(BF16)


def dot(a, b, contract=((1,), (0,))):
    return lax.dot_general(a, b, (contract, ((), ())), preferred_element_type=F32)


def dot3(a, b, contract=((1,), (0,))):
    return dot(a[0], b[0], contract) + (dot(a[0], b[1], contract) + dot(a[1], b[0], contract))


def lane_take(row, index):
    return jnp.take_along_axis(
        jnp.broadcast_to(row, index.shape), index, axis=1, mode="promise_in_bounds"
    )


def lane_number(rows):
    return lax.broadcasted_iota(jnp.int32, (rows, LANES), 1)


def take_columns(parts, lists):
    low = jnp.broadcast_to(lists & (LANES - 1), (SUBLANES, LANES))
    chunk = jnp.broadcast_to(lists >> 7, (SUBLANES, LANES))
    rows = []
    for base in range(0, 16, SUBLANES):
        value = jnp.take_along_axis(
            parts[0][base : base + SUBLANES], low, axis=1, mode="promise_in_bounds"
        )
        for number in range(1, len(parts)):
            other = jnp.take_along_axis(
                parts[number][base : base + SUBLANES], low, axis=1, mode="promise_in_bounds"
            )
            value = jnp.where(chunk == number, other, value)
        rows.append(value)
    return jnp.concatenate(rows, axis=0)


def add_columns(values, lists, columns):
    high, low = halves(values)
    places = lax.broadcasted_iota(jnp.int32, (columns, LANES), 0)
    hot = (places == jnp.broadcast_to(lists, (columns, LANES))).astype(F32).astype(BF16)
    summed = dot(jnp.concatenate([high, low], axis=0), hot, ((1,), (1,)))
    return summed[0:16] + summed[16:32]


def joined(lower, upper, row):
    lanes = lane_number(16)
    rows = lax.broadcasted_iota(jnp.int32, (16, LANES), 0)
    shift = jnp.where(rows == row, jnp.where(lanes < HALF, -BRICK, BRICK), 0.0)
    return jnp.where(lanes < HALF, lower, upper) + shift


def params_body(
    poly_ref, fit_ref, hidden_ref, bias_ref, out_ref, nb_ref,
    ws_ref, wst_ref, hid_ref, hidt_ref, cols_ref, nbt_ref,
    table, mixed, square, columns,
):
    table[...] = jnp.zeros_like(table)
    table[0:6, :] = poly_ref[0]
    table[6:12, :] = poly_ref[1] - poly_ref[0]
    features = table[...]
    split_features = halves(features)
    for n in range(M2):
        picked = fit_ref[pl.ds(n, HALF, stride=M2), :]
        mixed[pl.ds(n, 16, stride=M2), :] = dot3(split_features, halves(picked))
    axis_features = halves(features[:, 0:M2])
    for k in range(16):
        block = mixed[k * M2 : (k + 1) * M2, :]
        square[k * 16 : (k + 1) * 16, :] = dot3(axis_features, halves(block))
    for k in range(12):
        block = square[k * 16 : (k + 1) * 16, :] + square[pl.ds(k, 16, stride=16), :]
        ws_ref[k * 16 : (k + 1) * 16, :] = 0.5 * block
    ws_ref[192:256, :] = jnp.zeros((64, LANES), F32)
    wst_ref[:, 0:128] = ws_ref[0:128, :].T
    wst_ref[:, 128:256] = ws_ref[128:256, :].T
    for layer in range(2):
        high, low = halves(hidden_ref[layer])
        hid_ref[layer, 0] = high
        hid_ref[layer, 1] = low
        high, low = halves(hidden_ref[layer].T)
        hidt_ref[layer, 0] = high
        hidt_ref[layer, 1] = low
    columns[...] = jnp.zeros_like(columns)
    columns[0:3, :] = bias_ref[...]
    columns[3:4, :] = out_ref[...].reshape(1, LANES)
    cols_ref[...] = columns[...].T
    nbt_ref[...] = nb_ref[0, 0].T


def field_body(
    coords_hbm, types_hbm, cur_hbm, prev_hbm, send_x_hbm, send_y_hbm, spectrum_hbm,
    pack_ref, sent_ref, tail_ref,
    coords, types, cur, prev, send_x, send_y, spectrum, sems,
):
    pairs = (
        (coords_hbm, coords), (types_hbm, types), (cur_hbm, cur), (prev_hbm, prev),
        (send_x_hbm, send_x), (send_y_hbm, send_y), (spectrum_hbm, spectrum),
    )
    copies = [pltpu.make_async_copy(a, b, sems.at[n]) for n, (a, b) in enumerate(pairs)]
    for copy in copies:
        copy.start()
    for copy in copies:
        copy.wait()
    kind = types[0].astype(F32)
    scale = HEAVY + kind * (LIGHT - HEAVY)
    center = (spectrum[0] + spectrum[1]) / 2.0
    width = (spectrum[1] - spectrum[0]) / 2.0
    for a in range(3):
        pack_ref[a : a + 1, :] = coords[a, 0]
    pack_ref[3:4, :] = kind
    tail_ref[0:16, :] = jnp.broadcast_to(2.0 * scale / width, (16, LANES))
    tail_ref[0:3, :] = jnp.full((3, LANES), -1.0, F32)
    tail_ref[16:40, :] = jnp.zeros((24, LANES), F32)
    lanes = lane_number(1)
    sums = jnp.zeros((1, LANES), F32)
    for w in range(4):
        own = jnp.zeros((1, LANES), F32)
        old = jnp.zeros((1, LANES), F32)
        for b in range(3):
            current, past = cur[w, b, 0], prev[w, b, 0]
            own += current * current
            old += current * past
            row = 3 + 3 * w + b
            pack_ref[row + 1 : row + 2, :] = current * scale
            tail_ref[16 + row : 17 + row, :] = 2.0 * center * current / width + past
        own = jnp.sum(own, axis=1, keepdims=True)
        old = jnp.sum(old, axis=1, keepdims=True)
        sums = jnp.where(lanes == w, own, sums)
        sums = jnp.where(lanes == 4 + w, -2.0 * center / width * own - old, sums)
    lists_x = jnp.concatenate([send_x[0, 0, 1:2, :], send_x[0, 0, 0:1, :]], axis=1)
    lists_y = jnp.concatenate([send_y[0, 0, 1:2, :], send_y[0, 0, 0:1, :]], axis=1)
    pack_ref[16:24, :] = jnp.zeros((8, LANES), F32)
    pack_ref[16:17, :] = lists_y.astype(F32)
    pack_ref[17:18, :] = sums
    pack_ref[18:19, :] = jnp.full((1, LANES), 2.0 / width, F32)
    tail_ref[32:33, :] = lists_x.astype(F32)
    sent_ref[...] = take_columns([pack_ref[0:16, :]], lists_x)


def hold_body(pack_ref, held_ref):
    held_ref[...] = pack_ref[...]


def first_body(pack_ref, lower_ref, upper_ref, ghost_ref, sent_ref):
    ghost = joined(lower_ref[...], upper_ref[...], 0)
    ghost_ref[...] = ghost
    sent_ref[...] = take_columns([pack_ref[0:16, :], ghost], pack_ref[16:17, :].astype(jnp.int32))


def near_body(slots, pack_ref, ghost_ref, nbt_ref, near_ref):
    def body(group, carry):
        at = pl.ds(pl.multiple_of(group * SUBLANES, SUBLANES), SUBLANES)
        index = nbt_ref[at, :]
        low = index & (LANES - 1)
        second = (index >> 7) == 1
        for r in range(16):
            near_ref[r, at, :] = jnp.where(
                second, lane_take(ghost_ref[r : r + 1, :], low), lane_take(pack_ref[r : r + 1, :], low)
            )
        return carry

    lax.fori_loop(0, slots // SUBLANES, body, 0, unroll=2)


def pair_body(
    entries, slots,
    pack_ref, near_ref, lower_ref, upper_ref, nbt_ref,
    ws_ref, wst_ref, hid_ref, hidt_ref, cols_ref,
    accum_ref, share_ref,
    terms_ref, far, pair, power, moment, gee, form, back, lam,
):
    groups = slots // SUBLANES
    far[...] = joined(lower_ref[...], upper_ref[...], 1)
    moment[...] = jnp.zeros_like(moment)

    def gather(group, carry):
        at = pl.ds(pl.multiple_of(group * SUBLANES, SUBLANES), SUBLANES)
        index = nbt_ref[at, :]
        low = index & (LANES - 1)
        third = (index >> 7) == 2
        rows = []
        for r in range(16):
            value = jnp.where(third, lane_take(far[r : r + 1, :], low), near_ref[r, at, :])
            if r != 3:
                value = value - pack_ref[r : r + 1, :]
            pair[r, at, :] = value
            if r < 3:
                rows.append(value)
        x, y, z = rows
        radius_sq = x * x + y * y + z * z
        inverse = lax.rsqrt(radius_sq + SOFTENING)
        switch = 1.0 / (1.0 + radius_sq / CUTOFF_SQ)
        pair[16, at, :] = inverse
        value = switch
        for k in range(6):
            power[k, at, :] = value
            value = value * switch
        return carry

    lax.fori_loop(0, groups, gather, 0, unroll=2)

    zero = jnp.zeros((SUBLANES, LANES), F32)

    def sum_moments(w, parts):
        def body(group, totals):
            at = pl.ds(pl.multiple_of(group * SUBLANES, SUBLANES), SUBLANES)
            totals = list(totals)
            powers = [power[k, at, :] for k in range(6)]
            near = pair[3, at, :]
            inverse = pair[16, at, :]
            if w:
                d = [pair[a, at, :] for a in range(3)]
                v = [pair[1 + 3 * w + a, at, :] for a in range(3)]
                along = d[0] * v[0] + d[1] * v[1] + d[2] * v[2]
                tau = powers[0] * along * (-2.0 / CUTOFF_SQ)
                fall = inverse * inverse * along
            for place, c in enumerate(parts):
                if w == 0:
                    weight = None if c == 0 else pair[c - 1, at, :] * inverse
                elif c == 0:
                    weight, step = zero, tau
                else:
                    unit = d[c - 1] * inverse
                    step = tau * unit
                    weight = v[c - 1] * inverse - unit * fall
                for k in range(6):
                    if w:
                        weight = step if (c == 0 and k == 0) else weight + step
                    term = powers[k] if weight is None else powers[k] * weight
                    totals[place * 12 + k] += term
                    totals[place * 12 + 6 + k] += near * term
            return tuple(totals)

        totals = lax.fori_loop(0, groups, body, (zero,) * (12 * len(parts)), unroll=4)
        for place, c in enumerate(parts):
            for k in range(12):
                row = ((w * 4 + c) * 16 + k) * SUBLANES
                moment[row : row + SUBLANES, :] = totals[place * 12 + k]

    for w in range(5):
        sum_moments(w, (0, 1))
        sum_moments(w, (2, 3))

    for block in range(20):
        total = moment[pl.ds(block * 128, 16, stride=SUBLANES), :]
        for sub in range(1, SUBLANES):
            total += moment[pl.ds(block * 128 + sub, 16, stride=SUBLANES), :]
        gee[block] = total * (1.0 / slots)

    for k in range(12):
        for w in range(5):
            total = gee[w * 4] * gee[0, k : k + 1, :]
            for c in range(1, 4):
                total += gee[w * 4 + c] * gee[c, k : k + 1, :]
            form[k * 16 : (k + 1) * 16, w * LANES : (w + 1) * LANES] = total if w == 0 else total * 2.0
    form[192:256, :] = jnp.zeros((64, 5 * LANES), F32)

    def wide(column):
        return jnp.broadcast_to(column, (LANES, LANES))

    def cut(x, w):
        return x[:, w * LANES : (w + 1) * LANES]

    def layer(pre, bias):
        bent = jnp.tanh(cut(pre, 0) + wide(bias))
        slope = 1.0 - bent * bent
        return bent, slope

    pre1 = dot3(halves(wst_ref[...]), halves(form[...]))
    bent1, slope1 = layer(pre1, cols_ref[:, 0:1])
    hidden1 = [bent1] + [slope1 * cut(pre1, w) for w in range(1, 5)]
    pre2 = dot3((hidt_ref[0, 0], hidt_ref[0, 1]), halves(jnp.concatenate(hidden1, axis=1)))
    bent2, slope2 = layer(pre2, cols_ref[:, 1:2])
    hidden2 = [bent2 + hidden1[0]] + [slope2 * cut(pre2, w) + hidden1[w] for w in range(1, 5)]
    pre3 = dot3((hidt_ref[1, 0], hidt_ref[1, 1]), halves(jnp.concatenate(hidden2, axis=1)))
    bent3, slope3 = layer(pre3, cols_ref[:, 2:3])
    out = wide(cols_ref[:, 3:4])
    adj3 = [out * slope3] + [(-2.0 * out * bent3 * slope3) * cut(pre3, w) for w in range(1, 5)]
    up2 = dot3((hid_ref[1, 0], hid_ref[1, 1]), halves(jnp.concatenate(adj3, axis=1)))
    up2 = [cut(up2, 0) + out] + [cut(up2, w) for w in range(1, 5)]
    bend2 = -2.0 * up2[0] * bent2 * slope2
    adj2 = [up2[0] * slope2] + [up2[w] * slope2 + bend2 * cut(pre2, w) for w in range(1, 5)]
    up1 = dot3((hid_ref[0, 0], hid_ref[0, 1]), halves(jnp.concatenate(adj2, axis=1)))
    up1 = [cut(up1, w) + up2[w] for w in range(5)]
    bend1 = -2.0 * up1[0] * bent1 * slope1
    adj1 = [up1[0] * slope1] + [up1[w] * slope1 + bend1 * cut(pre1, w) for w in range(1, 5)]
    back[...] = dot3(halves(ws_ref[...]), halves(jnp.concatenate(adj1, axis=1)))

    for c in range(4):
        totals = [None] * 5
        for k in range(12):
            rows = slice(k * 16, (k + 1) * 16)
            base = back[rows, 0:LANES]
            plain = gee[c, k : k + 1, :]
            for w in range(5):
                if w == 0:
                    term = base * plain
                else:
                    term = back[rows, w * LANES : (w + 1) * LANES] * plain + base * gee[w * 4 + c, k : k + 1, :]
                totals[w] = term if k == 0 else totals[w] + term
        for w in range(5):
            lam[w * 4 + c] = totals[w] * (2.0 / slots)
            lam[w * 4 + c, 6:12, :] = lam[w * 4 + c, 0:6, :] + lam[w * 4 + c, 6:12, :]

    def push(group, quad):
        start = pl.multiple_of(group * SUBLANES, SUBLANES)
        at = pl.ds(start, SUBLANES)
        switch = power[0, at, :]
        inverse = pair[16, at, :]
        near = pair[3, at, :] > 0.5
        d = [pair[a, at, :] for a in range(3)]
        unit = [x * inverse for x in d]
        alpha = switch * (2.0 / CUTOFF_SQ)
        square = inverse * inverse
        quad = list(quad)

        def coefficients(w, c):
            return [
                jnp.where(near, lam[w * 4 + c, 6 + k : 7 + k, :], lam[w * 4 + c, k : k + 1, :])
                for k in range(6)
            ]

        def poly(values):
            total = values[5]
            for k in range(4, -1, -1):
                total = total * switch + values[k]
            return total * switch

        def store(row, value):
            terms_ref[pl.ds(start * 16 + row, SUBLANES, stride=16), :] = value

        plain, first, second = [], [], []
        for c in range(4):
            values = coefficients(0, c)
            plain.append(poly(values) if c else None)
            first.append(poly([values[k] * (k + 1.0) for k in range(6)]))
            second.append(poly([values[k] * ((k + 1.0) * (k + 1.0)) for k in range(6)]))

        def along(values):
            return values[1] * unit[0] + values[2] * unit[1] + values[3] * unit[2]

        plain_along = along(plain)
        first_along = along(first)
        first_sum = first[0] + first_along
        second_sum = second[0] + along(second)
        fall = -(alpha * first_sum + square * plain_along)
        for b in range(3):
            store(b, inverse * plain[b + 1] + d[b] * fall)
        bend = [-inverse * (square * plain[b + 1] + alpha * first[b + 1]) for b in range(3)]
        curl = (
            alpha * alpha * (first_sum + second_sum)
            + 2.0 * alpha * square * first_along
            + 3.0 * square * square * plain_along
        )
        for w in range(1, 5):
            values = [coefficients(w, c) for c in range(4)]
            p = [None] + [poly(values[c]) for c in range(1, 4)]
            f = [poly([values[c][k] * (k + 1.0) for k in range(6)]) for c in range(4)]
            down = -(alpha * (f[0] + along(f)) + square * along(p))
            v = [pair[1 + 3 * w + a, at, :] for a in range(3)]
            s = d[0] * v[0] + d[1] * v[1] + d[2] * v[2]
            t = s * curl + (bend[0] * v[0] + bend[1] * v[1] + bend[2] * v[2]) + down
            for b in range(3):
                term = bend[b] * s + v[b] * fall + d[b] * t + inverse * p[b + 1]
                store(3 * w + b, term)
                quad[w - 1] = quad[w - 1] + term * v[b]
        store(15, zero)
        return tuple(quad)

    quad = lax.fori_loop(0, groups, push, (zero,) * 4, unroll=2)

    lanes = lane_number(1)
    local = jnp.zeros((1, LANES), F32)
    for w in range(4):
        total = jnp.sum(jnp.sum(quad[w], axis=0, keepdims=True), axis=1, keepdims=True)
        local = jnp.where(lanes == 4 + w, total, local)
    share = (pack_ref[17:18, :] + pack_ref[18:19, :] * local) * (1.0 / entries)
    share_ref[...] = jnp.broadcast_to(share, share_ref.shape)
    total, own = scatter_columns(slots, terms_ref, nbt_ref)
    for c in range(3):
        part = total[c * 32 : c * 32 + 16] + total[c * 32 + 16 : c * 32 + 32]
        accum_ref[c] = part - own if c == 0 else part


def scatter_columns(slots, terms_ref, nbt_ref):
    per = 32
    places = lax.broadcasted_iota(jnp.int32, (LANES, LANES), 0)

    def body(group, carry):
        total, own = carry
        start = pl.multiple_of(group * per, per)
        lefts, rights = [], []
        for s in range(per):
            index = nbt_ref[pl.ds(start + s, 1), :]
            values = terms_ref[pl.ds((start + s) * 16, 16), :]
            own = own + values
            high, low = halves(values)
            chunk = index >> 7
            masks = [jnp.broadcast_to((chunk == c).astype(F32), (16, LANES)).astype(BF16) for c in range(3)]
            lefts.append(jnp.concatenate([x * m for m in masks for x in (high, low)], axis=0))
            hot = places == jnp.broadcast_to(index & (LANES - 1), (LANES, LANES))
            rights.append(hot.astype(F32).astype(BF16))
        left = jnp.concatenate(lefts, axis=1)
        right = jnp.concatenate(rights, axis=1)
        return total + dot(left, right, ((1,), (1,))), own

    start = (jnp.zeros((96, LANES), F32), jnp.zeros((16, LANES), F32))
    return lax.fori_loop(0, slots // per, body, start)


def fold_body(accum_ref, below_ref, above_ref, pack_ref, own_ref, ghost_ref):
    values = jnp.where(lane_number(16) < HALF, above_ref[...], below_ref[...])
    added = add_columns(values, pack_ref[16:17, :].astype(jnp.int32), 2 * LANES)
    own_ref[...] = accum_ref[0] + added[:, 0:LANES]
    ghost_ref[...] = accum_ref[1] + added[:, LANES:]


def last_body(
    own_ref, below_ref, above_ref, tail_ref, shares_ref,
    forces_ref, next_ref, moments_ref,
):
    values = jnp.where(lane_number(16) < HALF, above_ref[...], below_ref[...])
    own = own_ref[...] + add_columns(values, tail_ref[32:33, :].astype(jnp.int32), LANES)
    own = own * tail_ref[0:16, :] - tail_ref[16:32, :]
    for a in range(3):
        forces_ref[a, 0] = own[a : a + 1]
    for w in range(4):
        for b in range(3):
            row = 3 + 3 * w + b
            next_ref[w, b, 0] = own[row : row + 1]
    total = jnp.sum(shares_ref[...], axis=0, keepdims=True)
    moments_ref[0:1, :] = total[:, 0:4]
    moments_ref[1:2, :] = pltpu.roll(total, LANES - 4, 1)[:, 0:4]


def shifted(x, axis):
    devices = lax.axis_size(axis)
    up = [(i, (i + 1) % devices) for i in range(devices)]
    down = [(j, i) for i, j in up]
    return lax.ppermute(x, axis, up), lax.ppermute(x, axis, down)


def local(
    coords, atom_types, neighbours, send_x, send_y, poly_table, fit_in, fit_hidden, fit_bias,
    fit_out, spectrum, cheb_prev, cheb_cur,
):
    atoms, slots = neighbours.shape[2], neighbours.shape[3]
    devices = lax.axis_size("gx") * lax.axis_size("gy")
    entries = 3.0 * atoms * devices
    tile = shape(16, LANES)

    whole = (coords, atom_types, cheb_cur, cheb_prev, send_x, send_y)
    pack, sent, tail = call(
        field_body,
        [shape(24, LANES), tile, shape(40, LANES)],
        [pl.BlockSpec(memory_space=pltpu.HBM)] * 7,
        [pltpu.VMEM(x.shape, x.dtype) for x in whole]
        + [pltpu.SMEM(spectrum.shape, F32), pltpu.SemaphoreType.DMA((7,))],
        limit=None,
    )(*whole, spectrum)
    lower, upper = shifted(sent, "gx")
    pack = call(hold_body, shape(24, LANES), [VMEM], flops=4_000_000)(pack)
    ws, wst, hid, hidt, cols, nbt = call(
        params_body,
        [
            shape(256, LANES), shape(LANES, 256), shape(2, 2, 128, 128, dtype=BF16),
            shape(2, 2, 128, 128, dtype=BF16), shape(128, 128), shape(slots, atoms, dtype=jnp.int32),
        ],
        [VMEM] * 6,
        [pltpu.VMEM((16, HALF), F32), pltpu.VMEM((128, LANES), F32), pltpu.VMEM((256, LANES), F32), pltpu.VMEM((128, 128), F32)],
        flops=20_000_000,
    )(poly_table, fit_in, fit_hidden, fit_bias, fit_out, neighbours)
    ghost, sent = call(first_body, [tile, tile], [VMEM] * 3)(pack, lower, upper)
    lower, upper = shifted(sent, "gy")
    near = call(
        functools.partial(near_body, slots), shape(16, slots, LANES), [VMEM] * 3, flops=20_000_000
    )(pack, ghost, nbt)
    accum, share = call(
        functools.partial(pair_body, entries, slots),
        [shape(3, 16, LANES), shape(devices, LANES)],
        [VMEM] * 10,
        [
            pltpu.VMEM((slots * 16, LANES), F32),
            pltpu.VMEM((16, LANES), F32),
            pltpu.VMEM((17, slots, LANES), F32),
            pltpu.VMEM((6, slots, LANES), F32),
            pltpu.VMEM((20 * 128, LANES), F32),
            pltpu.VMEM((20, 16, LANES), F32),
            pltpu.VMEM((256, 5 * LANES), F32),
            pltpu.VMEM((256, 5 * LANES), F32),
            pltpu.VMEM((20, 16, LANES), F32),
        ],
        flops=40_000_000,
    )(pack, near, lower, upper, nbt, ws, wst, hid, hidt, cols)
    below, above = shifted(accum[2], "gy")
    shares = lax.all_to_all(share, ("gx", "gy"), 0, 0)
    own, ghost = call(fold_body, [tile, tile], [VMEM] * 4, flops=1000000000)(accum, below, above, pack)
    below, above = shifted(ghost, "gx")
    return tuple(
        call(
            last_body, [shape(*coords.shape), shape(*cheb_cur.shape), shape(2, 4)], [VMEM] * 5
        )(own, below, above, tail, shares)
    )


def solution(mesh):
    return jax.shard_map(
        local,
        mesh=mesh,
        in_specs=(
            P(None, "gx", "gy", None),
            P("gx", "gy", None),
            P("gx", "gy", None, None),
            P("gx", "gy", None, None),
            P("gx", "gy", None, None),
            P(),
            P(),
            P(),
            P(),
            P(),
            P(),
            P(None, None, "gx", "gy", None),
            P(None, None, "gx", "gy", None),
        ),
        out_specs=(P(None, "gx", "gy", None), P(None, None, "gx", "gy", None), P()),
        check_vma=False,
    )
```

```python
import functools

import jax
import jax.numpy as jnp
from jax import lax
from jax.experimental import pallas as pl
from jax.experimental.pallas import tpu as pltpu
from jax.sharding import PartitionSpec as P

BRICK = 5.0
SOFTENING = 0.25
CUTOFF_SQ = 16.0
LIGHT = 1.008 ** (-0.5)
HEAVY = 28.0855 ** (-0.5)
LANES = 128
SUBLANES = 8
M2 = 8
HALF = 64
F32 = jnp.float32
BF16 = jnp.bfloat16
VMEM = pl.BlockSpec(memory_space=pltpu.VMEM)


def shape(*dims, dtype=F32):
    return jax.ShapeDtypeStruct(dims, dtype)


def call(body, outs, specs, scratch=(), flops=0, limit=16 << 20):
    return pl.pallas_call(
        body,
        out_shape=outs,
        in_specs=specs,
        out_specs=jax.tree.map(lambda _: VMEM, outs),
        scratch_shapes=list(scratch),
        compiler_params=pltpu.CompilerParams(vmem_limit_bytes=limit),
        cost_estimate=pl.CostEstimate(flops=flops, bytes_accessed=1 << 16, transcendentals=0),
    )


def halves(x):
    high = x.astype(BF16)
    return high, (x - high.astype(F32)).astype(BF16)


def dot(a, b, contract=((1,), (0,))):
    return lax.dot_general(a, b, (contract, ((), ())), preferred_element_type=F32)


def dot3(a, b, contract=((1,), (0,))):
    return dot(a[0], b[0], contract) + (dot(a[0], b[1], contract) + dot(a[1], b[0], contract))


def deep_dot3(weights, x):
    high, low = halves(x)
    twice = jnp.concatenate([weights[0], weights[0]], axis=1)
    return dot(twice, jnp.concatenate([high, low], axis=0)) + dot(weights[1], high)


def lane_take(row, index):
    return jnp.take_along_axis(
        jnp.broadcast_to(row, index.shape), index, axis=1, mode="promise_in_bounds"
    )


def lane_number(rows):
    return lax.broadcasted_iota(jnp.int32, (rows, LANES), 1)


def take_columns(parts, lists):
    low = jnp.broadcast_to(lists & (LANES - 1), (SUBLANES, LANES))
    chunk = jnp.broadcast_to(lists >> 7, (SUBLANES, LANES))
    rows = []
    for base in range(0, 16, SUBLANES):
        value = jnp.take_along_axis(
            parts[0][base : base + SUBLANES], low, axis=1, mode="promise_in_bounds"
        )
        for number in range(1, len(parts)):
            other = jnp.take_along_axis(
                parts[number][base : base + SUBLANES], low, axis=1, mode="promise_in_bounds"
            )
            value = jnp.where(chunk == number, other, value)
        rows.append(value)
    return jnp.concatenate(rows, axis=0)


def add_columns(values, lists, columns):
    high, low = halves(values)
    places = lax.broadcasted_iota(jnp.int32, (columns, LANES), 0)
    hot = (places == jnp.broadcast_to(lists, (columns, LANES))).astype(F32).astype(BF16)
    summed = dot(jnp.concatenate([high, low], axis=0), hot, ((1,), (1,)))
    return summed[0:16] + summed[16:32]


def joined(lower, upper, row):
    lanes = lane_number(16)
    rows = lax.broadcasted_iota(jnp.int32, (16, LANES), 0)
    shift = jnp.where(rows == row, jnp.where(lanes < HALF, -BRICK, BRICK), 0.0)
    return jnp.where(lanes < HALF, lower, upper) + shift


def params_body(
    poly_ref, fit_ref, hidden_ref, bias_ref, out_ref, nb_ref,
    form_ref, back_ref, hid_ref, hidt_ref, cols_ref, nbt_ref,
    table, mixed, square, columns, even,
):
    table[...] = jnp.zeros_like(table)
    table[0:6, :] = poly_ref[0]
    table[6:12, :] = poly_ref[1] - poly_ref[0]
    features = table[...]
    split_features = halves(features)
    for n in range(M2):
        picked = fit_ref[pl.ds(n, HALF, stride=M2), :]
        mixed[pl.ds(n, 16, stride=M2), :] = dot3(split_features, halves(picked))
    axis_features = halves(features[:, 0:M2])
    for k in range(16):
        block = mixed[k * M2 : (k + 1) * M2, :]
        square[k * 16 : (k + 1) * 16, :] = dot3(axis_features, halves(block))
    for k in range(12):
        block = 0.5 * (square[k * 16 : (k + 1) * 16, :] + square[pl.ds(k, 16, stride=16), :])
        high, low = halves(block)
        back_ref[0, k * 16 : (k + 1) * 16, :] = high
        back_ref[1, k * 16 : (k + 1) * 16, :] = low
        if k < 8:
            even[k * 8 : (k + 1) * 8, :] = block[0:8]
        else:
            even[k * 8 : (k + 1) * 8, :] = 2.0 * block[0:8]
            even[(k + 4) * 8 : (k + 5) * 8, :] = block[8:16]
    high, low = halves(even[...].T)
    form_ref[0] = high
    form_ref[1] = low
    for layer in range(2):
        high, low = halves(hidden_ref[layer])
        hid_ref[layer, 0] = high
        hid_ref[layer, 1] = low
        high, low = halves(hidden_ref[layer].T)
        hidt_ref[layer, 0] = high
        hidt_ref[layer, 1] = low
    columns[...] = jnp.zeros_like(columns)
    columns[0:3, :] = bias_ref[...]
    columns[3:4, :] = out_ref[...].reshape(1, LANES)
    cols_ref[...] = columns[...].T
    nbt_ref[...] = nb_ref[0, 0].T


def field_body(
    coords_hbm, types_hbm, cur_hbm, prev_hbm, send_x_hbm, send_y_hbm, spectrum_hbm,
    pack_ref, sent_ref, tail_ref,
    coords, types, cur, prev, send_x, send_y, spectrum, sems,
):
    pairs = (
        (coords_hbm, coords), (types_hbm, types), (cur_hbm, cur), (prev_hbm, prev),
        (send_x_hbm, send_x), (send_y_hbm, send_y), (spectrum_hbm, spectrum),
    )
    copies = [pltpu.make_async_copy(a, b, sems.at[n]) for n, (a, b) in enumerate(pairs)]
    for copy in copies:
        copy.start()
    for copy in copies:
        copy.wait()
    kind = types[0].astype(F32)
    scale = HEAVY + kind * (LIGHT - HEAVY)
    center = (spectrum[0] + spectrum[1]) / 2.0
    width = (spectrum[1] - spectrum[0]) / 2.0
    for a in range(3):
        pack_ref[a : a + 1, :] = coords[a, 0]
    pack_ref[3:4, :] = kind
    tail_ref[0:16, :] = jnp.broadcast_to(2.0 * scale / width, (16, LANES))
    tail_ref[0:3, :] = jnp.full((3, LANES), -1.0, F32)
    tail_ref[16:40, :] = jnp.zeros((24, LANES), F32)
    lanes = lane_number(1)
    sums = jnp.zeros((1, LANES), F32)
    for w in range(4):
        own = jnp.zeros((1, LANES), F32)
        old = jnp.zeros((1, LANES), F32)
        for b in range(3):
            current, past = cur[w, b, 0], prev[w, b, 0]
            own += current * current
            old += current * past
            row = 3 + 3 * w + b
            pack_ref[row + 1 : row + 2, :] = current * scale
            tail_ref[16 + row : 17 + row, :] = 2.0 * center * current / width + past
        own = jnp.sum(own, axis=1, keepdims=True)
        old = jnp.sum(old, axis=1, keepdims=True)
        sums = jnp.where(lanes == w, own, sums)
        sums = jnp.where(lanes == 4 + w, -2.0 * center / width * own - old, sums)
    lists_x = jnp.concatenate([send_x[0, 0, 1:2, :], send_x[0, 0, 0:1, :]], axis=1)
    lists_y = jnp.concatenate([send_y[0, 0, 1:2, :], send_y[0, 0, 0:1, :]], axis=1)
    pack_ref[16:24, :] = jnp.zeros((8, LANES), F32)
    pack_ref[16:17, :] = lists_y.astype(F32)
    pack_ref[17:18, :] = sums
    pack_ref[18:19, :] = jnp.full((1, LANES), 2.0 / width, F32)
    tail_ref[32:33, :] = lists_x.astype(F32)
    sent_ref[...] = take_columns([pack_ref[0:16, :]], lists_x)


def hold_body(pack_ref, held_ref):
    held_ref[...] = pack_ref[...]


def first_body(pack_ref, upper_ref, lower_ref, ghost_ref, sent_ref):
    ghost = joined(lower_ref[...], upper_ref[...], 0)
    ghost_ref[...] = ghost
    sent_ref[...] = take_columns([pack_ref[0:16, :], ghost], pack_ref[16:17, :].astype(jnp.int32))


def near_body(slots, pack_ref, ghost_ref, nbt_ref, near_ref):
    def body(group, carry):
        at = pl.ds(pl.multiple_of(group * SUBLANES, SUBLANES), SUBLANES)
        index = nbt_ref[at, :]
        low = index & (LANES - 1)
        second = (index >> 7) == 1
        for r in range(16):
            near_ref[r, at, :] = jnp.where(
                second, lane_take(ghost_ref[r : r + 1, :], low), lane_take(pack_ref[r : r + 1, :], low)
            )
        return carry

    lax.fori_loop(0, slots // SUBLANES, body, 0, unroll=2)


def pair_body(
    entries, slots,
    pack_ref, near_ref, upper_ref, lower_ref, nbt_ref,
    form_ref, back_ref, hid_ref, hidt_ref, cols_ref,
    accum_ref, share_ref,
    terms_ref, far, pair, power, moment, gee, form, back, lam,
):
    groups = slots // SUBLANES
    far[...] = joined(lower_ref[...], upper_ref[...], 1)
    moment[...] = jnp.zeros_like(moment)

    def gather(group, carry):
        at = pl.ds(pl.multiple_of(group * SUBLANES, SUBLANES), SUBLANES)
        index = nbt_ref[at, :]
        low = index & (LANES - 1)
        third = (index >> 7) == 2
        rows = []
        for r in range(16):
            value = jnp.where(third, lane_take(far[r : r + 1, :], low), near_ref[r, at, :])
            if r != 3:
                value = value - pack_ref[r : r + 1, :]
            pair[r, at, :] = value
            if r < 3:
                rows.append(value)
        x, y, z = rows
        radius_sq = x * x + y * y + z * z
        inverse = lax.rsqrt(radius_sq + SOFTENING)
        switch = 1.0 / (1.0 + radius_sq / CUTOFF_SQ)
        pair[16, at, :] = inverse
        value = switch
        for k in range(6):
            power[k, at, :] = value
            value = value * switch
        return carry

    lax.fori_loop(0, groups, gather, 0, unroll=16)

    zero = jnp.zeros((SUBLANES, LANES), F32)

    def sum_moments(w, parts):
        def body(group, totals):
            at = pl.ds(pl.multiple_of(group * SUBLANES, SUBLANES), SUBLANES)
            totals = list(totals)
            powers = [power[k, at, :] for k in range(6)]
            near = pair[3, at, :]
            inverse = pair[16, at, :]
            if w:
                d = [pair[a, at, :] for a in range(3)]
                v = [pair[1 + 3 * w + a, at, :] for a in range(3)]
                along = d[0] * v[0] + d[1] * v[1] + d[2] * v[2]
                tau = powers[0] * along * (-2.0 / CUTOFF_SQ)
                fall = inverse * inverse * along
            for place, c in enumerate(parts):
                if w == 0:
                    weight = None if c == 0 else pair[c - 1, at, :] * inverse
                elif c == 0:
                    weight, step = zero, tau
                else:
                    unit = d[c - 1] * inverse
                    step = tau * unit
                    weight = v[c - 1] * inverse - unit * fall
                for k in range(6):
                    if w:
                        weight = step if (c == 0 and k == 0) else weight + step
                    term = powers[k] if weight is None else powers[k] * weight
                    totals[place * 12 + k] += term
                    totals[place * 12 + 6 + k] += near * term
            return tuple(totals)

        totals = lax.fori_loop(0, groups, body, (zero,) * (12 * len(parts)), unroll=16)
        for place, c in enumerate(parts):
            for k in range(12):
                row = ((w * 4 + c) * 16 + k) * SUBLANES
                moment[row : row + SUBLANES, :] = totals[place * 12 + k]

    for w in range(5):
        sum_moments(w, (0, 1))
        sum_moments(w, (2, 3))

    for block in range(20):
        total = moment[pl.ds(block * 128, 16, stride=SUBLANES), :]
        for sub in range(1, SUBLANES):
            total += moment[pl.ds(block * 128 + sub, 16, stride=SUBLANES), :]
        gee[block] = total * (1.0 / slots)

    for w in range(5):
        def product(k, rows):
            total = gee[w * 4, rows, :] * gee[0, k : k + 1, :]
            for c in range(1, 4):
                total += gee[w * 4 + c, rows, :] * gee[c, k : k + 1, :]
            return total

        def swapped(k, rows):
            total = gee[0, rows, :] * gee[w * 4, k : k + 1, :]
            for c in range(1, 4):
                total += gee[c, rows, :] * gee[w * 4 + c, k : k + 1, :]
            return total

        upper_rows, lower_rows = slice(0, 8), slice(8, 16)
        for k in range(12):
            block = product(k, upper_rows)
            if w:
                block = block + (swapped(k, upper_rows) if k >= 8 else block)
            form[k * 8 : (k + 1) * 8, w * LANES : (w + 1) * LANES] = block
            if k >= 8:
                block = product(k, lower_rows)
                form[(k + 4) * 8 : (k + 5) * 8, w * LANES : (w + 1) * LANES] = block * 2.0 if w else block

    def wide(column):
        return jnp.broadcast_to(column, (LANES, LANES))

    def cut(x, w):
        return x[:, w * LANES : (w + 1) * LANES]

    def layer(pre, bias):
        bent = jnp.tanh(cut(pre, 0) + wide(bias))
        slope = 1.0 - bent * bent
        return bent, slope

    pre1 = deep_dot3((form_ref[0], form_ref[1]), form[...])
    bent1, slope1 = layer(pre1, cols_ref[:, 0:1])
    hidden1 = [bent1] + [slope1 * cut(pre1, w) for w in range(1, 5)]
    pre2 = deep_dot3((hidt_ref[0, 0], hidt_ref[0, 1]), jnp.concatenate(hidden1, axis=1))
    bent2, slope2 = layer(pre2, cols_ref[:, 1:2])
    hidden2 = [bent2 + hidden1[0]] + [slope2 * cut(pre2, w) + hidden1[w] for w in range(1, 5)]
    pre3 = deep_dot3((hidt_ref[1, 0], hidt_ref[1, 1]), jnp.concatenate(hidden2, axis=1))
    bent3, slope3 = layer(pre3, cols_ref[:, 2:3])
    out = wide(cols_ref[:, 3:4])
    adj3 = [out * slope3] + [(-2.0 * out * bent3 * slope3) * cut(pre3, w) for w in range(1, 5)]
    up2 = deep_dot3((hid_ref[1, 0], hid_ref[1, 1]), jnp.concatenate(adj3, axis=1))
    up2 = [cut(up2, 0) + out] + [cut(up2, w) for w in range(1, 5)]
    bend2 = -2.0 * up2[0] * bent2 * slope2
    adj2 = [up2[0] * slope2] + [up2[w] * slope2 + bend2 * cut(pre2, w) for w in range(1, 5)]
    up1 = deep_dot3((hid_ref[0, 0], hid_ref[0, 1]), jnp.concatenate(adj2, axis=1))
    up1 = [cut(up1, w) + up2[w] for w in range(5)]
    bend1 = -2.0 * up1[0] * bent1 * slope1
    adj1 = [up1[0] * slope1] + [up1[w] * slope1 + bend1 * cut(pre1, w) for w in range(1, 5)]
    back[...] = deep_dot3((back_ref[0], back_ref[1]), jnp.concatenate(adj1, axis=1))

    rows = lax.broadcasted_iota(jnp.int32, (16, LANES), 0)
    degree = jnp.where(rows < 6, rows + 1, rows - 5).astype(F32)
    for c in range(4):
        totals = [None] * 5
        for k in range(12):
            rows = slice(k * 16, (k + 1) * 16)
            base = back[rows, 0:LANES]
            plain = gee[c, k : k + 1, :]
            for w in range(5):
                if w == 0:
                    term = base * plain
                else:
                    term = back[rows, w * LANES : (w + 1) * LANES] * plain + base * gee[w * 4 + c, k : k + 1, :]
                totals[w] = term if k == 0 else totals[w] + term
        for w in range(5):
            total = totals[w] * (2.0 / slots)
            lam[w * 4 + c] = total * degree if c == 0 else total
            lam[w * 4 + c, 6:12, :] = lam[w * 4 + c, 0:6, :] + lam[w * 4 + c, 6:12, :]

    def push(group, quad):
        start = pl.multiple_of(group * SUBLANES, SUBLANES)
        at = pl.ds(start, SUBLANES)
        switch = power[0, at, :]
        inverse = pair[16, at, :]
        near = pair[3, at, :] > 0.5
        d = [pair[a, at, :] for a in range(3)]
        unit = [x * inverse for x in d]
        alpha = switch * (2.0 / CUTOFF_SQ)
        square = inverse * inverse
        quad = list(quad)

        def coefficients(w, c):
            return [
                jnp.where(near, lam[w * 4 + c, 6 + k : 7 + k, :], lam[w * 4 + c, k : k + 1, :])
                for k in range(6)
            ]

        switch2 = switch * switch
        switch3 = switch2 * switch

        def horner(values, order):
            total, first, second = values[5], None, None
            for k in range(4, -1, -1):
                if order > 1 and first is not None:
                    second = first if second is None else second * switch + first
                if order > 0:
                    first = total if first is None else first * switch + total
                total = total * switch + values[k]
            return total, first, second

        def store(row, value):
            terms_ref[pl.ds(start * 16 + row, SUBLANES, stride=16), :] = value

        total, slope, _ = horner(coefficients(0, 0), 1)
        plain, first, second = [None], [switch * total], [switch * total + switch2 * slope]
        for c in range(1, 4):
            total, slope, bow = horner(coefficients(0, c), 2)
            total = switch * total
            slope = switch2 * slope
            plain.append(total)
            first.append(total + slope)
            second.append(total + 3.0 * slope + (2.0 * switch3) * bow)

        def along(values):
            return values[1] * unit[0] + values[2] * unit[1] + values[3] * unit[2]

        plain_along = along(plain)
        first_along = along(first)
        first_sum = first[0] + first_along
        second_sum = second[0] + along(second)
        fall = -(alpha * first_sum + square * plain_along)
        for b in range(3):
            store(b, inverse * plain[b + 1] + d[b] * fall)
        bend = [-inverse * (square * plain[b + 1] + alpha * first[b + 1]) for b in range(3)]
        curl = (
            alpha * alpha * (first_sum + second_sum)
            + 2.0 * alpha * square * first_along
            + 3.0 * square * square * plain_along
        )
        for w in range(1, 5):
            f0 = switch * horner(coefficients(w, 0), 0)[0]
            p, slopes = [None], [None]
            for c in range(1, 4):
                total, slope, _ = horner(coefficients(w, c), 1)
                p.append(switch * total)
                slopes.append(slope)
            p_along = along(p)
            down = -(alpha * (f0 + p_along + switch2 * along(slopes)) + square * p_along)
            v = [pair[1 + 3 * w + a, at, :] for a in range(3)]
            s = d[0] * v[0] + d[1] * v[1] + d[2] * v[2]
            t = s * curl + (bend[0] * v[0] + bend[1] * v[1] + bend[2] * v[2]) + down
            for b in range(3):
                term = bend[b] * s + v[b] * fall + d[b] * t + inverse * p[b + 1]
                store(3 * w + b, term)
                quad[w - 1] = quad[w - 1] + term * v[b]
        store(15, zero)
        return tuple(quad)

    quad = lax.fori_loop(0, groups, push, (zero,) * 4, unroll=2)

    lanes = lane_number(1)
    local = jnp.zeros((1, LANES), F32)
    for w in range(4):
        total = jnp.sum(jnp.sum(quad[w], axis=0, keepdims=True), axis=1, keepdims=True)
        local = jnp.where(lanes == 4 + w, total, local)
    share = (pack_ref[17:18, :] + pack_ref[18:19, :] * local) * (1.0 / entries)
    share_ref[...] = jnp.broadcast_to(share, share_ref.shape)
    total, own = scatter_columns(slots, terms_ref, nbt_ref)
    for c in range(3):
        part = total[c * 32 : c * 32 + 16] + total[c * 32 + 16 : c * 32 + 32]
        accum_ref[c] = part - own if c == 0 else part


def scatter_columns(slots, terms_ref, nbt_ref):
    per = 128
    places = lax.broadcasted_iota(jnp.int32, (LANES, LANES), 0)

    def body(group, carry):
        total, own = carry
        start = pl.multiple_of(group * per, per)
        lefts, rights = [], []
        for s in range(per):
            index = nbt_ref[pl.ds(start + s, 1), :]
            values = terms_ref[pl.ds((start + s) * 16, 16), :]
            own = own + values
            high, low = halves(values)
            chunk = index >> 7
            masks = [jnp.broadcast_to((chunk == c).astype(F32), (16, LANES)).astype(BF16) for c in range(3)]
            lefts.append(jnp.concatenate([x * m for m in masks for x in (high, low)], axis=0))
            hot = places == jnp.broadcast_to(index & (LANES - 1), (LANES, LANES))
            rights.append(hot.astype(F32).astype(BF16))
        left = jnp.concatenate(lefts, axis=1)
        right = jnp.concatenate(rights, axis=1)
        return total + dot(left, right, ((1,), (1,))), own

    start = (jnp.zeros((96, LANES), F32), jnp.zeros((16, LANES), F32))
    return lax.fori_loop(0, slots // per, body, start)


def fold_body(accum_ref, above_ref, below_ref, pack_ref, own_ref, ghost_ref):
    values = jnp.where(lane_number(16) < HALF, above_ref[...], below_ref[...])
    added = add_columns(values, pack_ref[16:17, :].astype(jnp.int32), 2 * LANES)
    own_ref[...] = accum_ref[0] + added[:, 0:LANES]
    ghost_ref[...] = accum_ref[1] + added[:, LANES:]


def last_body(
    own_ref, above_ref, below_ref, tail_ref, shares_ref,
    forces_ref, next_ref, moments_ref,
):
    values = jnp.where(lane_number(16) < HALF, above_ref[...], below_ref[...])
    own = own_ref[...] + add_columns(values, tail_ref[32:33, :].astype(jnp.int32), LANES)
    own = own * tail_ref[0:16, :] - tail_ref[16:32, :]
    for a in range(3):
        forces_ref[a, 0] = own[a : a + 1]
    for w in range(4):
        for b in range(3):
            row = 3 + 3 * w + b
            next_ref[w, b, 0] = own[row : row + 1]
    total = jnp.sum(shares_ref[...], axis=0, keepdims=True)
    moments_ref[0:1, :] = total[:, 0:4]
    moments_ref[1:2, :] = pltpu.roll(total, LANES - 4, 1)[:, 0:4]


def shifted(x, axis):
    devices = lax.axis_size(axis)
    up = [(i, (i + 1) % devices) for i in range(devices)]
    down = [(j, i) for i, j in up]
    return lax.ppermute(x, axis, up), lax.ppermute(x, axis, down)


def local(
    coords, atom_types, neighbours, send_x, send_y, poly_table, fit_in, fit_hidden, fit_bias,
    fit_out, spectrum, cheb_prev, cheb_cur,
):
    atoms, slots = neighbours.shape[2], neighbours.shape[3]
    devices = lax.axis_size("gx") * lax.axis_size("gy")
    entries = 3.0 * atoms * devices
    tile = shape(16, LANES)

    whole = (coords, atom_types, cheb_cur, cheb_prev, send_x, send_y)
    pack, sent, tail = call(
        field_body,
        [shape(24, LANES), tile, shape(40, LANES)],
        [pl.BlockSpec(memory_space=pltpu.HBM)] * 7,
        [pltpu.VMEM(x.shape, x.dtype) for x in whole]
        + [pltpu.SMEM(spectrum.shape, F32), pltpu.SemaphoreType.DMA((7,))],
        limit=None,
    )(*whole, spectrum)
    lower, upper = shifted(sent, "gx")
    pack = call(hold_body, shape(24, LANES), [VMEM], flops=4_000_000)(pack)
    forms, backs, hid, hidt, cols, nbt = call(
        params_body,
        [
            shape(2, 128, LANES, dtype=BF16), shape(2, 192, LANES, dtype=BF16), shape(2, 2, 128, 128, dtype=BF16),
            shape(2, 2, 128, 128, dtype=BF16), shape(128, 128), shape(slots, atoms, dtype=jnp.int32),
        ],
        [VMEM] * 6,
        [pltpu.VMEM((16, HALF), F32), pltpu.VMEM((128, LANES), F32), pltpu.VMEM((256, LANES), F32), pltpu.VMEM((128, 128), F32), pltpu.VMEM((128, LANES), F32)],
        flops=20_000_000,
    )(poly_table, fit_in, fit_hidden, fit_bias, fit_out, neighbours)
    ghost, sent = call(first_body, [tile, tile], [VMEM] * 3)(pack, upper, lower)
    lower, upper = shifted(sent, "gy")
    near = call(
        functools.partial(near_body, slots), shape(16, slots, LANES), [VMEM] * 3, flops=20_000_000
    )(pack, ghost, nbt)
    accum, share = call(
        functools.partial(pair_body, entries, slots),
        [shape(3, 16, LANES), shape(devices, LANES)],
        [VMEM] * 10,
        [
            pltpu.VMEM((slots * 16, LANES), F32),
            pltpu.VMEM((16, LANES), F32),
            pltpu.VMEM((17, slots, LANES), F32),
            pltpu.VMEM((6, slots, LANES), F32),
            pltpu.VMEM((20 * 128, LANES), F32),
            pltpu.VMEM((20, 16, LANES), F32),
            pltpu.VMEM((128, 5 * LANES), F32),
            pltpu.VMEM((192, 5 * LANES), F32),
            pltpu.VMEM((20, 16, LANES), F32),
        ],
        flops=40_000_000,
    )(pack, near, upper, lower, nbt, forms, backs, hid, hidt, cols)
    below, above = shifted(accum[2], "gy")
    shares = lax.all_to_all(share, ("gx", "gy"), 0, 0)
    own, ghost = call(fold_body, [tile, tile], [VMEM] * 4, flops=1000000000)(accum, above, below, pack)
    below, above = shifted(ghost, "gx")
    return tuple(
        call(
            last_body, [shape(*coords.shape), shape(*cheb_cur.shape), shape(2, 4)], [VMEM] * 5
        )(own, above, below, tail, shares)
    )


def solution(mesh):
    return jax.shard_map(
        local,
        mesh=mesh,
        in_specs=(
            P(None, "gx", "gy", None),
            P("gx", "gy", None),
            P("gx", "gy", None, None),
            P("gx", "gy", None, None),
            P("gx", "gy", None, None),
            P(),
            P(),
            P(),
            P(),
            P(),
            P(),
            P(None, None, "gx", "gy", None),
            P(None, None, "gx", "gy", None),
        ),
        out_specs=(P(None, "gx", "gy", None), P(None, None, "gx", "gy", None), P()),
        check_vma=False,
    )
```

```python
import functools

import jax
import jax.numpy as jnp
from jax import lax
from jax.experimental import pallas as pl
from jax.experimental.pallas import tpu as pltpu
from jax.sharding import PartitionSpec as P

BRICK = 5.0
SOFTENING = 0.25
CUTOFF_SQ = 16.0
LIGHT = 1.008 ** (-0.5)
HEAVY = 28.0855 ** (-0.5)
LANES = 128
SUBLANES = 8
M2 = 8
HALF = 64
F32 = jnp.float32
BF16 = jnp.bfloat16
VMEM = pl.BlockSpec(memory_space=pltpu.VMEM)


def shape(*dims, dtype=F32):
    return jax.ShapeDtypeStruct(dims, dtype)


def call(body, outs, specs, scratch=(), flops=0, limit=16 << 20):
    return pl.pallas_call(
        body,
        out_shape=outs,
        in_specs=specs,
        out_specs=jax.tree.map(lambda _: VMEM, outs),
        scratch_shapes=list(scratch),
        compiler_params=pltpu.CompilerParams(vmem_limit_bytes=limit),
        cost_estimate=pl.CostEstimate(flops=flops, bytes_accessed=1 << 16, transcendentals=0),
    )


def halves(x):
    high = x.astype(BF16)
    return high, (x - high.astype(F32)).astype(BF16)


def dot(a, b, contract=((1,), (0,))):
    return lax.dot_general(a, b, (contract, ((), ())), preferred_element_type=F32)


def dot3(a, b, contract=((1,), (0,))):
    return dot(a[0], b[0], contract) + (dot(a[0], b[1], contract) + dot(a[1], b[0], contract))


def deep_dot3(weights, x):
    high, low = halves(x)
    twice = jnp.concatenate([weights[0], weights[0]], axis=1)
    return dot(twice, jnp.concatenate([high, low], axis=0)) + dot(weights[1], high)


def lane_take(row, index):
    return jnp.take_along_axis(
        jnp.broadcast_to(row, index.shape), index, axis=1, mode="promise_in_bounds"
    )


def lane_number(rows):
    return lax.broadcasted_iota(jnp.int32, (rows, LANES), 1)


def take_columns(parts, lists):
    low = jnp.broadcast_to(lists & (LANES - 1), (SUBLANES, LANES))
    chunk = jnp.broadcast_to(lists >> 7, (SUBLANES, LANES))
    rows = []
    for base in range(0, 16, SUBLANES):
        value = jnp.take_along_axis(
            parts[0][base : base + SUBLANES], low, axis=1, mode="promise_in_bounds"
        )
        for number in range(1, len(parts)):
            other = jnp.take_along_axis(
                parts[number][base : base + SUBLANES], low, axis=1, mode="promise_in_bounds"
            )
            value = jnp.where(chunk == number, other, value)
        rows.append(value)
    return jnp.concatenate(rows, axis=0)


def add_columns(values, lists, columns):
    high, low = halves(values)
    places = lax.broadcasted_iota(jnp.int32, (columns, LANES), 0)
    hot = (places == jnp.broadcast_to(lists, (columns, LANES))).astype(F32).astype(BF16)
    summed = dot(jnp.concatenate([high, low], axis=0), hot, ((1,), (1,)))
    return summed[0:16] + summed[16:32]


def joined(lower, upper, row):
    lanes = lane_number(16)
    rows = lax.broadcasted_iota(jnp.int32, (16, LANES), 0)
    shift = jnp.where(rows == row, jnp.where(lanes < HALF, -BRICK, BRICK), 0.0)
    return jnp.where(lanes < HALF, lower, upper) + shift


def params_body(
    poly_ref, fit_ref, hidden_ref, bias_ref, out_ref, nb_ref, pack_ref,
    held_ref, form_ref, back_ref, hid_ref, hidt_ref, cols_ref, nbt_ref,
    table, mixed, square, columns, even,
):
    table[...] = jnp.zeros_like(table)
    table[0:6, :] = poly_ref[0]
    table[6:12, :] = poly_ref[1] - poly_ref[0]
    features = table[...]
    split_features = halves(features)
    for n in range(M2):
        picked = fit_ref[pl.ds(n, HALF, stride=M2), :]
        mixed[pl.ds(n, 16, stride=M2), :] = dot3(split_features, halves(picked))
    axis_features = halves(features[:, 0:M2])
    for k in range(16):
        block = mixed[k * M2 : (k + 1) * M2, :]
        square[k * 16 : (k + 1) * 16, :] = dot3(axis_features, halves(block))
    for k in range(12):
        block = 0.5 * (square[k * 16 : (k + 1) * 16, :] + square[pl.ds(k, 16, stride=16), :])
        high, low = halves(block)
        back_ref[0, k * 16 : (k + 1) * 16, :] = high
        back_ref[1, k * 16 : (k + 1) * 16, :] = low
        if k < 8:
            even[k * 8 : (k + 1) * 8, :] = block[0:8]
        else:
            even[k * 8 : (k + 1) * 8, :] = 2.0 * block[0:8]
            even[(k + 4) * 8 : (k + 5) * 8, :] = block[8:16]
    high, low = halves(even[...].T)
    form_ref[0] = high
    form_ref[1] = low
    for layer in range(2):
        high, low = halves(hidden_ref[layer])
        hid_ref[layer, 0] = high
        hid_ref[layer, 1] = low
        high, low = halves(hidden_ref[layer].T)
        hidt_ref[layer, 0] = high
        hidt_ref[layer, 1] = low
    columns[...] = jnp.zeros_like(columns)
    columns[0:3, :] = bias_ref[...]
    columns[3:4, :] = out_ref[...].reshape(1, LANES)
    cols_ref[...] = columns[...].T
    nbt_ref[...] = nb_ref[0, 0].T
    held_ref[...] = pack_ref[...]


def field_body(
    coords_hbm, types_hbm, cur_hbm, prev_hbm, send_x_hbm, send_y_hbm, spectrum_hbm,
    pack_ref, sent_ref, tail_ref,
    coords, types, cur, prev, send_x, send_y, spectrum, sems,
):
    pairs = (
        (coords_hbm, coords), (types_hbm, types), (cur_hbm, cur), (prev_hbm, prev),
        (send_x_hbm, send_x), (send_y_hbm, send_y), (spectrum_hbm, spectrum),
    )
    copies = [pltpu.make_async_copy(a, b, sems.at[n]) for n, (a, b) in enumerate(pairs)]
    for copy in copies:
        copy.start()
    for copy in copies:
        copy.wait()
    kind = types[0].astype(F32)
    scale = HEAVY + kind * (LIGHT - HEAVY)
    center = (spectrum[0] + spectrum[1]) / 2.0
    width = (spectrum[1] - spectrum[0]) / 2.0
    for a in range(3):
        pack_ref[a : a + 1, :] = coords[a, 0]
    pack_ref[3:4, :] = kind
    tail_ref[0:16, :] = jnp.broadcast_to(2.0 * scale / width, (16, LANES))
    tail_ref[0:3, :] = jnp.full((3, LANES), -1.0, F32)
    tail_ref[16:40, :] = jnp.zeros((24, LANES), F32)
    lanes = lane_number(1)
    sums = jnp.zeros((1, LANES), F32)
    for w in range(4):
        own = jnp.zeros((1, LANES), F32)
        old = jnp.zeros((1, LANES), F32)
        for b in range(3):
            current, past = cur[w, b, 0], prev[w, b, 0]
            own += current * current
            old += current * past
            row = 3 + 3 * w + b
            pack_ref[row + 1 : row + 2, :] = current * scale
            tail_ref[16 + row : 17 + row, :] = 2.0 * center * current / width + past
        own = jnp.sum(own, axis=1, keepdims=True)
        old = jnp.sum(old, axis=1, keepdims=True)
        sums = jnp.where(lanes == w, own, sums)
        sums = jnp.where(lanes == 4 + w, -2.0 * center / width * own - old, sums)
    lists_x = jnp.concatenate([send_x[0, 0, 1:2, :], send_x[0, 0, 0:1, :]], axis=1)
    lists_y = jnp.concatenate([send_y[0, 0, 1:2, :], send_y[0, 0, 0:1, :]], axis=1)
    pack_ref[16:24, :] = jnp.zeros((8, LANES), F32)
    pack_ref[16:17, :] = lists_y.astype(F32)
    pack_ref[17:18, :] = sums
    pack_ref[18:19, :] = jnp.full((1, LANES), 2.0 / width, F32)
    tail_ref[32:33, :] = lists_x.astype(F32)
    sent_ref[...] = take_columns([pack_ref[0:16, :]], lists_x)


def first_body(pack_ref, upper_ref, lower_ref, ghost_ref, sent_ref):
    ghost = joined(lower_ref[...], upper_ref[...], 0)
    ghost_ref[...] = ghost
    sent_ref[...] = take_columns([pack_ref[0:16, :], ghost], pack_ref[16:17, :].astype(jnp.int32))


def near_body(slots, pack_ref, ghost_ref, nbt_ref, near_ref):
    def body(group, carry):
        at = pl.ds(pl.multiple_of(group * SUBLANES, SUBLANES), SUBLANES)
        index = nbt_ref[at, :]
        low = index & (LANES - 1)
        second = (index >> 7) == 1
        for r in range(16):
            near_ref[r, at, :] = jnp.where(
                second, lane_take(ghost_ref[r : r + 1, :], low), lane_take(pack_ref[r : r + 1, :], low)
            )
        return carry

    lax.fori_loop(0, slots // SUBLANES, body, 0, unroll=2)


def pair_body(
    entries, slots,
    pack_ref, near_ref, upper_ref, lower_ref, nbt_ref,
    form_ref, back_ref, hid_ref, hidt_ref, cols_ref,
    accum_ref, share_ref,
    terms_ref, far, pair, power, moment, gee, form, back, lam,
):
    groups = slots // SUBLANES
    far[...] = joined(lower_ref[...], upper_ref[...], 1)
    moment[...] = jnp.zeros_like(moment)

    def gather(group, carry):
        at = pl.ds(pl.multiple_of(group * SUBLANES, SUBLANES), SUBLANES)
        index = nbt_ref[at, :]
        low = index & (LANES - 1)
        third = (index >> 7) == 2
        rows = []
        for r in range(16):
            value = jnp.where(third, lane_take(far[r : r + 1, :], low), near_ref[r, at, :])
            if r != 3:
                value = value - pack_ref[r : r + 1, :]
            pair[r, at, :] = value
            if r < 3:
                rows.append(value)
        x, y, z = rows
        radius_sq = x * x + y * y + z * z
        inverse = lax.rsqrt(radius_sq + SOFTENING)
        switch = 1.0 / (1.0 + radius_sq / CUTOFF_SQ)
        pair[16, at, :] = inverse
        value = switch
        for k in range(6):
            power[k, at, :] = value
            value = value * switch
        return carry

    lax.fori_loop(0, groups, gather, 0, unroll=16)

    zero = jnp.zeros((SUBLANES, LANES), F32)

    def sum_moments(w, parts):
        def body(group, totals):
            at = pl.ds(pl.multiple_of(group * SUBLANES, SUBLANES), SUBLANES)
            totals = list(totals)
            powers = [power[k, at, :] for k in range(6)]
            near = pair[3, at, :]
            inverse = pair[16, at, :]
            if w:
                d = [pair[a, at, :] for a in range(3)]
                v = [pair[1 + 3 * w + a, at, :] for a in range(3)]
                along = d[0] * v[0] + d[1] * v[1] + d[2] * v[2]
                tau = powers[0] * along * (-2.0 / CUTOFF_SQ)
                fall = inverse * inverse * along
            for place, c in enumerate(parts):
                if w == 0:
                    weight = None if c == 0 else pair[c - 1, at, :] * inverse
                elif c == 0:
                    weight, step = zero, tau
                else:
                    unit = d[c - 1] * inverse
                    step = tau * unit
                    weight = v[c - 1] * inverse - unit * fall
                for k in range(6):
                    if w:
                        weight = step if (c == 0 and k == 0) else weight + step
                    term = powers[k] if weight is None else powers[k] * weight
                    totals[place * 12 + k] += term
                    totals[place * 12 + 6 + k] += near * term
            return tuple(totals)

        totals = lax.fori_loop(0, groups, body, (zero,) * (12 * len(parts)), unroll=16)
        for place, c in enumerate(parts):
            for k in range(12):
                row = ((w * 4 + c) * 16 + k) * SUBLANES
                moment[row : row + SUBLANES, :] = totals[place * 12 + k]

    for w in range(5):
        sum_moments(w, (0, 1))
        sum_moments(w, (2, 3))

    for block in range(20):
        total = moment[pl.ds(block * 128, 16, stride=SUBLANES), :]
        for sub in range(1, SUBLANES):
            total += moment[pl.ds(block * 128 + sub, 16, stride=SUBLANES), :]
        gee[block] = total * (1.0 / slots)

    for w in range(5):
        def product(k, rows):
            total = gee[w * 4, rows, :] * gee[0, k : k + 1, :]
            for c in range(1, 4):
                total += gee[w * 4 + c, rows, :] * gee[c, k : k + 1, :]
            return total

        def swapped(k, rows):
            total = gee[0, rows, :] * gee[w * 4, k : k + 1, :]
            for c in range(1, 4):
                total += gee[c, rows, :] * gee[w * 4 + c, k : k + 1, :]
            return total

        upper_rows, lower_rows = slice(0, 8), slice(8, 16)
        for k in range(12):
            block = product(k, upper_rows)
            if w:
                block = block + (swapped(k, upper_rows) if k >= 8 else block)
            form[k * 8 : (k + 1) * 8, w * LANES : (w + 1) * LANES] = block
            if k >= 8:
                block = product(k, lower_rows)
                form[(k + 4) * 8 : (k + 5) * 8, w * LANES : (w + 1) * LANES] = block * 2.0 if w else block

    def wide(column):
        return jnp.broadcast_to(column, (LANES, LANES))

    def cut(x, w):
        return x[:, w * LANES : (w + 1) * LANES]

    def layer(pre, bias):
        bent = jnp.tanh(cut(pre, 0) + wide(bias))
        slope = 1.0 - bent * bent
        return bent, slope

    pre1 = deep_dot3((form_ref[0], form_ref[1]), form[...])
    bent1, slope1 = layer(pre1, cols_ref[:, 0:1])
    hidden1 = [bent1] + [slope1 * cut(pre1, w) for w in range(1, 5)]
    pre2 = deep_dot3((hidt_ref[0, 0], hidt_ref[0, 1]), jnp.concatenate(hidden1, axis=1))
    bent2, slope2 = layer(pre2, cols_ref[:, 1:2])
    hidden2 = [bent2 + hidden1[0]] + [slope2 * cut(pre2, w) + hidden1[w] for w in range(1, 5)]
    pre3 = deep_dot3((hidt_ref[1, 0], hidt_ref[1, 1]), jnp.concatenate(hidden2, axis=1))
    bent3, slope3 = layer(pre3, cols_ref[:, 2:3])
    out = wide(cols_ref[:, 3:4])
    adj3 = [out * slope3] + [(-2.0 * out * bent3 * slope3) * cut(pre3, w) for w in range(1, 5)]
    up2 = deep_dot3((hid_ref[1, 0], hid_ref[1, 1]), jnp.concatenate(adj3, axis=1))
    up2 = [cut(up2, 0) + out] + [cut(up2, w) for w in range(1, 5)]
    bend2 = -2.0 * up2[0] * bent2 * slope2
    adj2 = [up2[0] * slope2] + [up2[w] * slope2 + bend2 * cut(pre2, w) for w in range(1, 5)]
    up1 = deep_dot3((hid_ref[0, 0], hid_ref[0, 1]), jnp.concatenate(adj2, axis=1))
    up1 = [cut(up1, w) + up2[w] for w in range(5)]
    bend1 = -2.0 * up1[0] * bent1 * slope1
    adj1 = [up1[0] * slope1] + [up1[w] * slope1 + bend1 * cut(pre1, w) for w in range(1, 5)]
    back[...] = deep_dot3((back_ref[0], back_ref[1]), jnp.concatenate(adj1, axis=1))

    rows = lax.broadcasted_iota(jnp.int32, (16, LANES), 0)
    degree = jnp.where(rows < 6, rows + 1, rows - 5).astype(F32)
    for c in range(4):
        totals = [None] * 5
        for k in range(12):
            rows = slice(k * 16, (k + 1) * 16)
            base = back[rows, 0:LANES]
            plain = gee[c, k : k + 1, :]
            for w in range(5):
                if w == 0:
                    term = base * plain
                else:
                    term = back[rows, w * LANES : (w + 1) * LANES] * plain + base * gee[w * 4 + c, k : k + 1, :]
                totals[w] = term if k == 0 else totals[w] + term
        for w in range(5):
            total = totals[w] * (2.0 / slots)
            lam[w * 4 + c] = total * degree if c == 0 else total
            lam[w * 4 + c, 6:12, :] = lam[w * 4 + c, 0:6, :] + lam[w * 4 + c, 6:12, :]

    def push(group, quad):
        start = pl.multiple_of(group * SUBLANES, SUBLANES)
        at = pl.ds(start, SUBLANES)
        switch = power[0, at, :]
        inverse = pair[16, at, :]
        near = pair[3, at, :] > 0.5
        d = [pair[a, at, :] for a in range(3)]
        unit = [x * inverse for x in d]
        alpha = switch * (2.0 / CUTOFF_SQ)
        square = inverse * inverse
        quad = list(quad)

        def coefficients(w, c):
            return [
                jnp.where(near, lam[w * 4 + c, 6 + k : 7 + k, :], lam[w * 4 + c, k : k + 1, :])
                for k in range(6)
            ]

        switch2 = switch * switch
        switch3 = switch2 * switch

        def horner(values, order):
            total, first, second = values[5], None, None
            for k in range(4, -1, -1):
                if order > 1 and first is not None:
                    second = first if second is None else second * switch + first
                if order > 0:
                    first = total if first is None else first * switch + total
                total = total * switch + values[k]
            return total, first, second

        def store(row, value):
            terms_ref[pl.ds(start * 16 + row, SUBLANES, stride=16), :] = value

        total, slope, _ = horner(coefficients(0, 0), 1)
        plain, first, second = [None], [switch * total], [switch * total + switch2 * slope]
        for c in range(1, 4):
            total, slope, bow = horner(coefficients(0, c), 2)
            total = switch * total
            slope = switch2 * slope
            plain.append(total)
            first.append(total + slope)
            second.append(total + 3.0 * slope + (2.0 * switch3) * bow)

        def along(values):
            return values[1] * unit[0] + values[2] * unit[1] + values[3] * unit[2]

        plain_along = along(plain)
        first_along = along(first)
        first_sum = first[0] + first_along
        second_sum = second[0] + along(second)
        fall = -(alpha * first_sum + square * plain_along)
        for b in range(3):
            store(b, inverse * plain[b + 1] + d[b] * fall)
        bend = [-inverse * (square * plain[b + 1] + alpha * first[b + 1]) for b in range(3)]
        curl = (
            alpha * alpha * (first_sum + second_sum)
            + 2.0 * alpha * square * first_along
            + 3.0 * square * square * plain_along
        )
        for w in range(1, 5):
            f0 = switch * horner(coefficients(w, 0), 0)[0]
            p, slopes = [None], [None]
            for c in range(1, 4):
                total, slope, _ = horner(coefficients(w, c), 1)
                p.append(switch * total)
                slopes.append(slope)
            p_along = along(p)
            down = -(alpha * (f0 + p_along + switch2 * along(slopes)) + square * p_along)
            v = [pair[1 + 3 * w + a, at, :] for a in range(3)]
            s = d[0] * v[0] + d[1] * v[1] + d[2] * v[2]
            t = s * curl + (bend[0] * v[0] + bend[1] * v[1] + bend[2] * v[2]) + down
            for b in range(3):
                term = bend[b] * s + v[b] * fall + d[b] * t + inverse * p[b + 1]
                store(3 * w + b, term)
                quad[w - 1] = quad[w - 1] + term * v[b]
        store(15, zero)
        return tuple(quad)

    quad = lax.fori_loop(0, groups, push, (zero,) * 4, unroll=2)

    lanes = lane_number(1)
    local = jnp.zeros((1, LANES), F32)
    for w in range(4):
        total = jnp.sum(jnp.sum(quad[w], axis=0, keepdims=True), axis=1, keepdims=True)
        local = jnp.where(lanes == 4 + w, total, local)
    share = (pack_ref[17:18, :] + pack_ref[18:19, :] * local) * (1.0 / entries)
    share_ref[...] = jnp.broadcast_to(share, share_ref.shape)
    total, own = scatter_columns(slots, terms_ref, nbt_ref)
    for c in range(3):
        part = total[c * 32 : c * 32 + 16] + total[c * 32 + 16 : c * 32 + 32]
        accum_ref[c] = part - own if c == 0 else part


def scatter_columns(slots, terms_ref, nbt_ref):
    per = 128
    places = lax.broadcasted_iota(jnp.int32, (LANES, LANES), 0)

    def body(group, carry):
        total, own = carry
        start = pl.multiple_of(group * per, per)
        lefts, rights = [], []
        for s in range(per):
            index = nbt_ref[pl.ds(start + s, 1), :]
            values = terms_ref[pl.ds((start + s) * 16, 16), :]
            own = own + values
            high, low = halves(values)
            chunk = index >> 7
            masks = [jnp.broadcast_to((chunk == c).astype(F32), (16, LANES)).astype(BF16) for c in range(3)]
            lefts.append(jnp.concatenate([x * m for m in masks for x in (high, low)], axis=0))
            hot = places == jnp.broadcast_to(index & (LANES - 1), (LANES, LANES))
            rights.append(hot.astype(F32).astype(BF16))
        left = jnp.concatenate(lefts, axis=1)
        right = jnp.concatenate(rights, axis=1)
        return total + dot(left, right, ((1,), (1,))), own

    start = (jnp.zeros((96, LANES), F32), jnp.zeros((16, LANES), F32))
    return lax.fori_loop(0, slots // per, body, start)


def fold_body(accum_ref, above_ref, below_ref, pack_ref, own_ref, ghost_ref):
    values = jnp.where(lane_number(16) < HALF, above_ref[...], below_ref[...])
    added = add_columns(values, pack_ref[16:17, :].astype(jnp.int32), 2 * LANES)
    own_ref[...] = accum_ref[0] + added[:, 0:LANES]
    ghost_ref[...] = accum_ref[1] + added[:, LANES:]


def last_body(
    own_ref, above_ref, below_ref, tail_ref, shares_ref,
    forces_ref, next_ref, moments_ref,
):
    values = jnp.where(lane_number(16) < HALF, above_ref[...], below_ref[...])
    own = own_ref[...] + add_columns(values, tail_ref[32:33, :].astype(jnp.int32), LANES)
    own = own * tail_ref[0:16, :] - tail_ref[16:32, :]
    for a in range(3):
        forces_ref[a, 0] = own[a : a + 1]
    for w in range(4):
        for b in range(3):
            row = 3 + 3 * w + b
            next_ref[w, b, 0] = own[row : row + 1]
    total = jnp.sum(shares_ref[...], axis=0, keepdims=True)
    moments_ref[0:1, :] = total[:, 0:4]
    moments_ref[1:2, :] = pltpu.roll(total, LANES - 4, 1)[:, 0:4]


def shifted(x, axis):
    devices = lax.axis_size(axis)
    up = [(i, (i + 1) % devices) for i in range(devices)]
    down = [(j, i) for i, j in up]
    return lax.ppermute(x, axis, up), lax.ppermute(x, axis, down)


def local(
    coords, atom_types, neighbours, send_x, send_y, poly_table, fit_in, fit_hidden, fit_bias,
    fit_out, spectrum, cheb_prev, cheb_cur,
):
    atoms, slots = neighbours.shape[2], neighbours.shape[3]
    devices = lax.axis_size("gx") * lax.axis_size("gy")
    entries = 3.0 * atoms * devices
    tile = shape(16, LANES)

    whole = (coords, atom_types, cheb_cur, cheb_prev, send_x, send_y)
    pack, sent, tail = call(
        field_body,
        [shape(24, LANES), tile, shape(40, LANES)],
        [pl.BlockSpec(memory_space=pltpu.HBM)] * 7,
        [pltpu.VMEM(x.shape, x.dtype) for x in whole]
        + [pltpu.SMEM(spectrum.shape, F32), pltpu.SemaphoreType.DMA((7,))],
        limit=None,
        flops=2_000_000_000,
    )(*whole, spectrum)
    lower, upper = shifted(sent, "gx")
    pack, forms, backs, hid, hidt, cols, nbt = call(
        params_body,
        [
            shape(24, LANES), shape(2, 128, LANES, dtype=BF16), shape(2, 192, LANES, dtype=BF16), shape(2, 2, 128, 128, dtype=BF16),
            shape(2, 2, 128, 128, dtype=BF16), shape(128, 128), shape(slots, atoms, dtype=jnp.int32),
        ],
        [VMEM] * 7,
        [pltpu.VMEM((16, HALF), F32), pltpu.VMEM((128, LANES), F32), pltpu.VMEM((256, LANES), F32), pltpu.VMEM((128, 128), F32), pltpu.VMEM((128, LANES), F32)],
        flops=20_000_000,
    )(poly_table, fit_in, fit_hidden, fit_bias, fit_out, neighbours, pack)
    ghost, sent = call(first_body, [tile, tile], [VMEM] * 3, flops=2_000_000_000)(pack, upper, lower)
    lower, upper = shifted(sent, "gy")
    near = call(
        functools.partial(near_body, slots), shape(16, slots, LANES), [VMEM] * 3, flops=20_000_000
    )(pack, ghost, nbt)
    accum, share = call(
        functools.partial(pair_body, entries, slots),
        [shape(3, 16, LANES), shape(devices, LANES)],
        [VMEM] * 10,
        [
            pltpu.VMEM((slots * 16, LANES), F32),
            pltpu.VMEM((16, LANES), F32),
            pltpu.VMEM((17, slots, LANES), F32),
            pltpu.VMEM((6, slots, LANES), F32),
            pltpu.VMEM((20 * 128, LANES), F32),
            pltpu.VMEM((20, 16, LANES), F32),
            pltpu.VMEM((128, 5 * LANES), F32),
            pltpu.VMEM((192, 5 * LANES), F32),
            pltpu.VMEM((20, 16, LANES), F32),
        ],
        flops=40_000_000,
    )(pack, near, upper, lower, nbt, forms, backs, hid, hidt, cols)
    below, above = shifted(accum[2], "gy")
    shares = lax.all_to_all(share, ("gx", "gy"), 0, 0)
    own, ghost = call(fold_body, [tile, tile], [VMEM] * 4, flops=1000000000)(accum, above, below, pack)
    below, above = shifted(ghost, "gx")
    return tuple(
        call(
            last_body, [shape(*coords.shape), shape(*cheb_cur.shape), shape(2, 4)], [VMEM] * 5
        )(own, above, below, tail, shares)
    )


def solution(mesh):
    return jax.shard_map(
        local,
        mesh=mesh,
        in_specs=(
            P(None, "gx", "gy", None),
            P("gx", "gy", None),
            P("gx", "gy", None, None),
            P("gx", "gy", None, None),
            P("gx", "gy", None, None),
            P(),
            P(),
            P(),
            P(),
            P(),
            P(),
            P(None, None, "gx", "gy", None),
            P(None, None, "gx", "gy", None),
        ),
        out_specs=(P(None, "gx", "gy", None), P(None, None, "gx", "gy", None), P()),
        check_vma=False,
    )
```

```python
import functools

import jax
import jax.numpy as jnp
from jax import lax
from jax.experimental import pallas as pl
from jax.experimental.pallas import tpu as pltpu
from jax.sharding import PartitionSpec as P

BRICK = 5.0
SOFTENING = 0.25
CUTOFF_SQ = 16.0
LIGHT = 1.008 ** (-0.5)
HEAVY = 28.0855 ** (-0.5)
LANES = 128
SUBLANES = 8
M2 = 8
HALF = 64
F32 = jnp.float32
BF16 = jnp.bfloat16
VMEM = pl.BlockSpec(memory_space=pltpu.VMEM)


def shape(*dims, dtype=F32):
    return jax.ShapeDtypeStruct(dims, dtype)


def call(body, outs, specs, scratch=(), flops=0, limit=16 << 20, places=None):
    return pl.pallas_call(
        body,
        out_shape=outs,
        in_specs=specs,
        out_specs=places or jax.tree.map(lambda _: VMEM, outs),
        scratch_shapes=list(scratch),
        compiler_params=pltpu.CompilerParams(vmem_limit_bytes=limit),
        cost_estimate=pl.CostEstimate(flops=flops, bytes_accessed=1 << 16, transcendentals=0),
    )


def halves(x):
    high = x.astype(BF16)
    return high, (x - high.astype(F32)).astype(BF16)


def dot(a, b, contract=((1,), (0,))):
    return lax.dot_general(a, b, (contract, ((), ())), preferred_element_type=F32)


def dot3(a, b, contract=((1,), (0,))):
    return dot(a[0], b[0], contract) + (dot(a[0], b[1], contract) + dot(a[1], b[0], contract))


def deep_dot3(weights, x):
    high, low = halves(x)
    twice = jnp.concatenate([weights[0], weights[0]], axis=1)
    return dot(twice, jnp.concatenate([high, low], axis=0)) + dot(weights[1], high)


def lane_take(row, index):
    return jnp.take_along_axis(
        jnp.broadcast_to(row, index.shape), index, axis=1, mode="promise_in_bounds"
    )


def lane_number(rows):
    return lax.broadcasted_iota(jnp.int32, (rows, LANES), 1)


def take_columns(parts, lists):
    low = jnp.broadcast_to(lists & (LANES - 1), (SUBLANES, LANES))
    chunk = jnp.broadcast_to(lists >> 7, (SUBLANES, LANES))
    rows = []
    for base in range(0, 16, SUBLANES):
        value = jnp.take_along_axis(
            parts[0][base : base + SUBLANES], low, axis=1, mode="promise_in_bounds"
        )
        for number in range(1, len(parts)):
            other = jnp.take_along_axis(
                parts[number][base : base + SUBLANES], low, axis=1, mode="promise_in_bounds"
            )
            value = jnp.where(chunk == number, other, value)
        rows.append(value)
    return jnp.concatenate(rows, axis=0)


def add_columns(values, lists, columns):
    high, low = halves(values)
    places = lax.broadcasted_iota(jnp.int32, (columns, LANES), 0)
    hot = (places == jnp.broadcast_to(lists, (columns, LANES))).astype(F32).astype(BF16)
    summed = dot(jnp.concatenate([high, low], axis=0), hot, ((1,), (1,)))
    return summed[0:16] + summed[16:32]


def joined(lower, upper, row):
    lanes = lane_number(16)
    rows = lax.broadcasted_iota(jnp.int32, (16, LANES), 0)
    shift = jnp.where(rows == row, jnp.where(lanes < HALF, -BRICK, BRICK), 0.0)
    return jnp.where(lanes < HALF, lower, upper) + shift


def params_body(
    poly_ref, fit_ref, hidden_ref, bias_ref, out_ref, nb_ref, pack_ref,
    held_ref, form_ref, back_ref, hid_ref, hidt_ref, cols_ref, nbt_ref,
    table, mixed, square, columns, even,
):
    table[...] = jnp.zeros_like(table)
    table[0:6, :] = poly_ref[0]
    table[6:12, :] = poly_ref[1] - poly_ref[0]
    features = table[...]
    split_features = halves(features)
    for n in range(M2):
        picked = fit_ref[pl.ds(n, HALF, stride=M2), :]
        mixed[pl.ds(n, 16, stride=M2), :] = dot3(split_features, halves(picked))
    axis_features = halves(features[:, 0:M2])
    for k in range(16):
        block = mixed[k * M2 : (k + 1) * M2, :]
        square[k * 16 : (k + 1) * 16, :] = dot3(axis_features, halves(block))
    for k in range(12):
        block = 0.5 * (square[k * 16 : (k + 1) * 16, :] + square[pl.ds(k, 16, stride=16), :])
        high, low = halves(block)
        back_ref[0, k * 16 : (k + 1) * 16, :] = high
        back_ref[1, k * 16 : (k + 1) * 16, :] = low
        if k < 8:
            even[k * 8 : (k + 1) * 8, :] = block[0:8]
        else:
            even[k * 8 : (k + 1) * 8, :] = 2.0 * block[0:8]
            even[(k + 4) * 8 : (k + 5) * 8, :] = block[8:16]
    high, low = halves(even[...].T)
    form_ref[0] = high
    form_ref[1] = low
    for layer in range(2):
        high, low = halves(hidden_ref[layer])
        hid_ref[layer, 0] = high
        hid_ref[layer, 1] = low
        high, low = halves(hidden_ref[layer].T)
        hidt_ref[layer, 0] = high
        hidt_ref[layer, 1] = low
    columns[...] = jnp.zeros_like(columns)
    columns[0:3, :] = bias_ref[...]
    columns[3:4, :] = out_ref[...].reshape(1, LANES)
    cols_ref[...] = columns[...].T
    nbt_ref[...] = nb_ref[0, 0].T
    held_ref[...] = pack_ref[...]


def field_body(
    coords_hbm, types_hbm, cur_hbm, prev_hbm, send_x_hbm, send_y_hbm, spectrum_hbm,
    pack_ref, sent_ref, tail_ref,
    coords, types, cur, prev, send_x, send_y, spectrum, sems,
):
    pairs = (
        (coords_hbm, coords), (types_hbm, types), (cur_hbm, cur), (prev_hbm, prev),
        (send_x_hbm, send_x), (send_y_hbm, send_y), (spectrum_hbm, spectrum),
    )
    copies = [pltpu.make_async_copy(a, b, sems.at[n]) for n, (a, b) in enumerate(pairs)]
    for copy in copies:
        copy.start()
    for copy in copies:
        copy.wait()
    kind = types[0].astype(F32)
    scale = HEAVY + kind * (LIGHT - HEAVY)
    center = (spectrum[0] + spectrum[1]) / 2.0
    width = (spectrum[1] - spectrum[0]) / 2.0
    for a in range(3):
        pack_ref[a : a + 1, :] = coords[a, 0]
    pack_ref[3:4, :] = kind
    tail_ref[0:16, :] = jnp.broadcast_to(2.0 * scale / width, (16, LANES))
    tail_ref[0:3, :] = jnp.full((3, LANES), -1.0, F32)
    tail_ref[16:40, :] = jnp.zeros((24, LANES), F32)
    lanes = lane_number(1)
    sums = jnp.zeros((1, LANES), F32)
    for w in range(4):
        own = jnp.zeros((1, LANES), F32)
        old = jnp.zeros((1, LANES), F32)
        for b in range(3):
            current, past = cur[w, b, 0], prev[w, b, 0]
            own += current * current
            old += current * past
            row = 3 + 3 * w + b
            pack_ref[row + 1 : row + 2, :] = current * scale
            tail_ref[16 + row : 17 + row, :] = 2.0 * center * current / width + past
        own = jnp.sum(own, axis=1, keepdims=True)
        old = jnp.sum(old, axis=1, keepdims=True)
        sums = jnp.where(lanes == w, own, sums)
        sums = jnp.where(lanes == 4 + w, -2.0 * center / width * own - old, sums)
    lists_x = jnp.concatenate([send_x[0, 0, 1:2, :], send_x[0, 0, 0:1, :]], axis=1)
    lists_y = jnp.concatenate([send_y[0, 0, 1:2, :], send_y[0, 0, 0:1, :]], axis=1)
    pack_ref[16:24, :] = jnp.zeros((8, LANES), F32)
    pack_ref[16:17, :] = lists_y.astype(F32)
    pack_ref[17:18, :] = sums
    pack_ref[18:19, :] = jnp.full((1, LANES), 2.0 / width, F32)
    tail_ref[32:33, :] = lists_x.astype(F32)
    sent_ref[...] = take_columns([pack_ref[0:16, :]], lists_x)


def first_body(pack_ref, upper_ref, lower_ref, ghost_ref, sent_ref):
    ghost = joined(lower_ref[...], upper_ref[...], 0)
    ghost_ref[...] = ghost
    sent_ref[...] = take_columns([pack_ref[0:16, :], ghost], pack_ref[16:17, :].astype(jnp.int32))


def near_body(slots, pack_ref, ghost_ref, nbt_ref, near_ref):
    def body(group, carry):
        at = pl.ds(pl.multiple_of(group * SUBLANES, SUBLANES), SUBLANES)
        index = nbt_ref[at, :]
        low = index & (LANES - 1)
        second = (index >> 7) == 1
        for r in range(16):
            near_ref[r, at, :] = jnp.where(
                second, lane_take(ghost_ref[r : r + 1, :], low), lane_take(pack_ref[r : r + 1, :], low)
            )
        return carry

    lax.fori_loop(0, slots // SUBLANES, body, 0, unroll=2)


def pair_body(
    entries, slots,
    pack_ref, near_ref, upper_ref, lower_ref, nbt_ref,
    form_ref, back_ref, hid_ref, hidt_ref, cols_ref,
    accum_ref, share_ref,
    terms_ref, far, pair, power, moment, gee, form, back, lam, share_vmem, sem,
):
    groups = slots // SUBLANES
    far[...] = joined(lower_ref[...], upper_ref[...], 1)
    for block in range(20):
        moment[block * 128 + 96 : (block + 1) * 128, :] = jnp.zeros((32, LANES), F32)

    def gather(group, carry):
        at = pl.ds(pl.multiple_of(group * SUBLANES, SUBLANES), SUBLANES)
        index = nbt_ref[at, :]
        low = index & (LANES - 1)
        third = (index >> 7) == 2
        rows = []
        for r in range(16):
            value = jnp.where(third, lane_take(far[r : r + 1, :], low), near_ref[r, at, :])
            if r != 3:
                value = value - pack_ref[r : r + 1, :]
            pair[r, at, :] = value
            if r < 3:
                rows.append(value)
        x, y, z = rows
        radius_sq = x * x + y * y + z * z
        inverse = lax.rsqrt(radius_sq + SOFTENING)
        switch = 1.0 / (1.0 + radius_sq / CUTOFF_SQ)
        pair[16, at, :] = inverse
        value = switch
        for k in range(6):
            power[k, at, :] = value
            value = value * switch
        return carry

    lax.fori_loop(0, groups, gather, 0, unroll=16)

    zero = jnp.zeros((SUBLANES, LANES), F32)

    def sum_moments(w, parts):
        def body(group, totals):
            at = pl.ds(pl.multiple_of(group * SUBLANES, SUBLANES), SUBLANES)
            totals = list(totals)
            powers = [power[k, at, :] for k in range(6)]
            near = pair[3, at, :]
            inverse = pair[16, at, :]
            if w:
                d = [pair[a, at, :] for a in range(3)]
                v = [pair[1 + 3 * w + a, at, :] for a in range(3)]
                along = d[0] * v[0] + d[1] * v[1] + d[2] * v[2]
                tau = powers[0] * along * (-2.0 / CUTOFF_SQ)
                fall = inverse * inverse * along
            for place, c in enumerate(parts):
                if w == 0:
                    weight = None if c == 0 else pair[c - 1, at, :] * inverse
                elif c == 0:
                    weight, step = zero, tau
                else:
                    unit = d[c - 1] * inverse
                    step = tau * unit
                    weight = v[c - 1] * inverse - unit * fall
                for k in range(6):
                    if w:
                        weight = step if (c == 0 and k == 0) else weight + step
                    term = powers[k] if weight is None else powers[k] * weight
                    totals[place * 12 + k] += term
                    totals[place * 12 + 6 + k] += near * term
            return tuple(totals)

        totals = lax.fori_loop(0, groups, body, (zero,) * (12 * len(parts)), unroll=16)
        for place, c in enumerate(parts):
            for k in range(12):
                row = ((w * 4 + c) * 16 + k) * SUBLANES
                moment[row : row + SUBLANES, :] = totals[place * 12 + k]

    for w in range(5):
        sum_moments(w, (0, 1))
        sum_moments(w, (2, 3))

    for block in range(20):
        total = moment[pl.ds(block * 128, 16, stride=SUBLANES), :]
        for sub in range(1, SUBLANES):
            total += moment[pl.ds(block * 128 + sub, 16, stride=SUBLANES), :]
        gee[block] = total * (1.0 / slots)

    for w in range(5):
        def product(k, rows):
            total = gee[w * 4, rows, :] * gee[0, k : k + 1, :]
            for c in range(1, 4):
                total += gee[w * 4 + c, rows, :] * gee[c, k : k + 1, :]
            return total

        def swapped(k, rows):
            total = gee[0, rows, :] * gee[w * 4, k : k + 1, :]
            for c in range(1, 4):
                total += gee[c, rows, :] * gee[w * 4 + c, k : k + 1, :]
            return total

        upper_rows, lower_rows = slice(0, 8), slice(8, 16)
        for k in range(12):
            block = product(k, upper_rows)
            if w:
                block = block + (swapped(k, upper_rows) if k >= 8 else block)
            form[k * 8 : (k + 1) * 8, w * LANES : (w + 1) * LANES] = block
            if k >= 8:
                block = product(k, lower_rows)
                form[(k + 4) * 8 : (k + 5) * 8, w * LANES : (w + 1) * LANES] = block * 2.0 if w else block

    def wide(column):
        return jnp.broadcast_to(column, (LANES, LANES))

    def cut(x, w):
        return x[:, w * LANES : (w + 1) * LANES]

    def layer(pre, bias):
        bent = jnp.tanh(cut(pre, 0) + wide(bias))
        slope = 1.0 - bent * bent
        return bent, slope

    pre1 = deep_dot3((form_ref[0], form_ref[1]), form[...])
    bent1, slope1 = layer(pre1, cols_ref[:, 0:1])
    hidden1 = [bent1] + [slope1 * cut(pre1, w) for w in range(1, 5)]
    pre2 = deep_dot3((hidt_ref[0, 0], hidt_ref[0, 1]), jnp.concatenate(hidden1, axis=1))
    bent2, slope2 = layer(pre2, cols_ref[:, 1:2])
    hidden2 = [bent2 + hidden1[0]] + [slope2 * cut(pre2, w) + hidden1[w] for w in range(1, 5)]
    pre3 = deep_dot3((hidt_ref[1, 0], hidt_ref[1, 1]), jnp.concatenate(hidden2, axis=1))
    bent3, slope3 = layer(pre3, cols_ref[:, 2:3])
    out = wide(cols_ref[:, 3:4])
    adj3 = [out * slope3] + [(-2.0 * out * bent3 * slope3) * cut(pre3, w) for w in range(1, 5)]
    up2 = deep_dot3((hid_ref[1, 0], hid_ref[1, 1]), jnp.concatenate(adj3, axis=1))
    up2 = [cut(up2, 0) + out] + [cut(up2, w) for w in range(1, 5)]
    bend2 = -2.0 * up2[0] * bent2 * slope2
    adj2 = [up2[0] * slope2] + [up2[w] * slope2 + bend2 * cut(pre2, w) for w in range(1, 5)]
    up1 = deep_dot3((hid_ref[0, 0], hid_ref[0, 1]), jnp.concatenate(adj2, axis=1))
    up1 = [cut(up1, w) + up2[w] for w in range(5)]
    bend1 = -2.0 * up1[0] * bent1 * slope1
    adj1 = [up1[0] * slope1] + [up1[w] * slope1 + bend1 * cut(pre1, w) for w in range(1, 5)]
    back[...] = deep_dot3((back_ref[0], back_ref[1]), jnp.concatenate(adj1, axis=1))

    rows = lax.broadcasted_iota(jnp.int32, (16, LANES), 0)
    degree = jnp.where(rows < 6, rows + 1, rows - 5).astype(F32)
    for c in range(4):
        totals = [None] * 5
        for k in range(12):
            rows = slice(k * 16, (k + 1) * 16)
            base = back[rows, 0:LANES]
            plain = gee[c, k : k + 1, :]
            for w in range(5):
                if w == 0:
                    term = base * plain
                else:
                    term = back[rows, w * LANES : (w + 1) * LANES] * plain + base * gee[w * 4 + c, k : k + 1, :]
                totals[w] = term if k == 0 else totals[w] + term
        for w in range(5):
            total = totals[w] * (2.0 / slots)
            lam[w * 4 + c] = total * degree if c == 0 else total
            lam[w * 4 + c, 6:12, :] = lam[w * 4 + c, 0:6, :] + lam[w * 4 + c, 6:12, :]

    def push(group, quad):
        start = pl.multiple_of(group * SUBLANES, SUBLANES)
        at = pl.ds(start, SUBLANES)
        switch = power[0, at, :]
        inverse = pair[16, at, :]
        near = pair[3, at, :] > 0.5
        d = [pair[a, at, :] for a in range(3)]
        unit = [x * inverse for x in d]
        alpha = switch * (2.0 / CUTOFF_SQ)
        square = inverse * inverse
        quad = list(quad)

        def coefficients(w, c):
            return [
                jnp.where(near, lam[w * 4 + c, 6 + k : 7 + k, :], lam[w * 4 + c, k : k + 1, :])
                for k in range(6)
            ]

        switch2 = switch * switch
        switch3 = switch2 * switch

        def horner(values, order):
            total, first, second = values[5], None, None
            for k in range(4, -1, -1):
                if order > 1 and first is not None:
                    second = first if second is None else second * switch + first
                if order > 0:
                    first = total if first is None else first * switch + total
                total = total * switch + values[k]
            return total, first, second

        def store(row, value):
            terms_ref[pl.ds(start * 16 + row, SUBLANES, stride=16), :] = value

        total, slope, _ = horner(coefficients(0, 0), 1)
        plain, first, second = [None], [switch * total], [switch * total + switch2 * slope]
        for c in range(1, 4):
            total, slope, bow = horner(coefficients(0, c), 2)
            total = switch * total
            slope = switch2 * slope
            plain.append(total)
            first.append(total + slope)
            second.append(total + 3.0 * slope + (2.0 * switch3) * bow)

        def along(values):
            return values[1] * unit[0] + values[2] * unit[1] + values[3] * unit[2]

        plain_along = along(plain)
        first_along = along(first)
        first_sum = first[0] + first_along
        second_sum = second[0] + along(second)
        fall = -(alpha * first_sum + square * plain_along)
        for b in range(3):
            store(b, inverse * plain[b + 1] + d[b] * fall)
        bend = [-inverse * (square * plain[b + 1] + alpha * first[b + 1]) for b in range(3)]
        curl = (
            alpha * alpha * (first_sum + second_sum)
            + 2.0 * alpha * square * first_along
            + 3.0 * square * square * plain_along
        )
        for w in range(1, 5):
            f0 = switch * horner(coefficients(w, 0), 0)[0]
            p, slopes = [None], [None]
            for c in range(1, 4):
                total, slope, _ = horner(coefficients(w, c), 1)
                p.append(switch * total)
                slopes.append(slope)
            p_along = along(p)
            down = -(alpha * (f0 + p_along + switch2 * along(slopes)) + square * p_along)
            v = [pair[1 + 3 * w + a, at, :] for a in range(3)]
            s = d[0] * v[0] + d[1] * v[1] + d[2] * v[2]
            t = s * curl + (bend[0] * v[0] + bend[1] * v[1] + bend[2] * v[2]) + down
            for b in range(3):
                term = bend[b] * s + v[b] * fall + d[b] * t + inverse * p[b + 1]
                store(3 * w + b, term)
                quad[w - 1] = quad[w - 1] + term * v[b]
        store(15, zero)
        return tuple(quad)

    quad = lax.fori_loop(0, groups, push, (zero,) * 4, unroll=2)

    lanes = lane_number(1)
    local = jnp.zeros((1, LANES), F32)
    for w in range(4):
        total = jnp.sum(jnp.sum(quad[w], axis=0, keepdims=True), axis=1, keepdims=True)
        local = jnp.where(lanes == 4 + w, total, local)
    share = (pack_ref[17:18, :] + pack_ref[18:19, :] * local) * (1.0 / entries)
    share_vmem[...] = jnp.broadcast_to(share, share_vmem.shape)
    copy = pltpu.make_async_copy(share_vmem, share_ref, sem)
    copy.start()
    total, own = scatter_columns(slots, terms_ref, nbt_ref)
    for c in range(3):
        part = total[c * 32 : c * 32 + 16] + total[c * 32 + 16 : c * 32 + 32]
        accum_ref[c] = part - own if c == 0 else part
    copy.wait()


def scatter_columns(slots, terms_ref, nbt_ref):
    per = 64
    places = lax.broadcasted_iota(jnp.int32, (LANES, LANES), 0)

    def body(group, carry):
        total, own = carry
        start = pl.multiple_of(group * per, per)
        lefts, rights = [], []
        for s in range(per):
            index = nbt_ref[pl.ds(start + s, 1), :]
            values = terms_ref[pl.ds((start + s) * 16, 16), :]
            own = own + values
            high, low = halves(values)
            chunk = index >> 7
            masks = [jnp.broadcast_to((chunk == c).astype(F32), (16, LANES)).astype(BF16) for c in range(3)]
            lefts.append(jnp.concatenate([x * m for m in masks for x in (high, low)], axis=0))
            hot = places == jnp.broadcast_to(index & (LANES - 1), (LANES, LANES))
            rights.append(hot.astype(F32).astype(BF16))
        left = jnp.concatenate(lefts, axis=1)
        right = jnp.concatenate(rights, axis=1)
        return total + dot(left, right, ((1,), (1,))), own

    start = (jnp.zeros((96, LANES), F32), jnp.zeros((16, LANES), F32))
    return lax.fori_loop(0, slots // per, body, start)


def fold_body(accum_ref, above_ref, below_ref, pack_ref, own_ref, ghost_ref):
    values = jnp.where(lane_number(16) < HALF, above_ref[...], below_ref[...])
    added = add_columns(values, pack_ref[16:17, :].astype(jnp.int32), 2 * LANES)
    own_ref[...] = accum_ref[0] + added[:, 0:LANES]
    ghost_ref[...] = accum_ref[1] + added[:, LANES:]


def last_body(
    own_ref, above_ref, below_ref, tail_ref,
    forces_ref, next_ref,
):
    values = jnp.where(lane_number(16) < HALF, above_ref[...], below_ref[...])
    own = own_ref[...] + add_columns(values, tail_ref[32:33, :].astype(jnp.int32), LANES)
    own = own * tail_ref[0:16, :] - tail_ref[16:32, :]
    for a in range(3):
        forces_ref[a, 0] = own[a : a + 1]
    for w in range(4):
        for b in range(3):
            row = 3 + 3 * w + b
            next_ref[w, b, 0] = own[row : row + 1]


def moments_body(shares_ref, moments_ref):
    total = jnp.sum(shares_ref[...], axis=0, keepdims=True)
    moments_ref[0:1, :] = total[:, 0:4]
    moments_ref[1:2, :] = pltpu.roll(total, LANES - 4, 1)[:, 0:4]


def shifted(x, axis):
    devices = lax.axis_size(axis)
    up = [(i, (i + 1) % devices) for i in range(devices)]
    down = [(j, i) for i, j in up]
    return lax.ppermute(x, axis, up), lax.ppermute(x, axis, down)


def local(
    coords, atom_types, neighbours, send_x, send_y, poly_table, fit_in, fit_hidden, fit_bias,
    fit_out, spectrum, cheb_prev, cheb_cur,
):
    atoms, slots = neighbours.shape[2], neighbours.shape[3]
    devices = lax.axis_size("gx") * lax.axis_size("gy")
    entries = 3.0 * atoms * devices
    tile = shape(16, LANES)

    whole = (coords, atom_types, cheb_cur, cheb_prev, send_x, send_y)
    pack, sent, tail = call(
        field_body,
        [shape(24, LANES), tile, shape(40, LANES)],
        [pl.BlockSpec(memory_space=pltpu.HBM)] * 7,
        [pltpu.VMEM(x.shape, x.dtype) for x in whole]
        + [pltpu.SMEM(spectrum.shape, F32), pltpu.SemaphoreType.DMA((7,))],
        limit=None,
        flops=2_000_000_000,
    )(*whole, spectrum)
    lower, upper = shifted(sent, "gx")
    pack, forms, backs, hid, hidt, cols, nbt = call(
        params_body,
        [
            shape(24, LANES), shape(2, 128, LANES, dtype=BF16), shape(2, 192, LANES, dtype=BF16), shape(2, 2, 128, 128, dtype=BF16),
            shape(2, 2, 128, 128, dtype=BF16), shape(128, 128), shape(slots, atoms, dtype=jnp.int32),
        ],
        [VMEM] * 7,
        [pltpu.VMEM((16, HALF), F32), pltpu.VMEM((128, LANES), F32), pltpu.VMEM((256, LANES), F32), pltpu.VMEM((128, 128), F32), pltpu.VMEM((128, LANES), F32)],
        flops=20_000_000,
    )(poly_table, fit_in, fit_hidden, fit_bias, fit_out, neighbours, pack)
    ghost, sent = call(first_body, [tile, tile], [VMEM] * 3, flops=2_000_000_000)(pack, upper, lower)
    lower, upper = shifted(sent, "gy")
    near = call(
        functools.partial(near_body, slots), shape(16, slots, LANES), [VMEM] * 3, flops=20_000_000
    )(pack, ghost, nbt)
    accum, share = call(
        functools.partial(pair_body, entries, slots),
        [shape(3, 16, LANES), shape(devices, LANES)],
        [VMEM] * 10,
        [
            pltpu.VMEM((slots * 16, LANES), F32),
            pltpu.VMEM((16, LANES), F32),
            pltpu.VMEM((17, slots, LANES), F32),
            pltpu.VMEM((6, slots, LANES), F32),
            pltpu.VMEM((20 * 128, LANES), F32),
            pltpu.VMEM((20, 16, LANES), F32),
            pltpu.VMEM((128, 5 * LANES), F32),
            pltpu.VMEM((192, 5 * LANES), F32),
            pltpu.VMEM((20, 16, LANES), F32),
            pltpu.VMEM((devices, LANES), F32),
            pltpu.SemaphoreType.DMA,
        ],
        flops=40_000_000,
        places=[VMEM, pl.BlockSpec(memory_space=pl.ANY)],
    )(pack, near, upper, lower, nbt, forms, backs, hid, hidt, cols)
    below, above = shifted(accum[2], "gy")
    shares = lax.all_to_all(share, ("gx", "gy"), 0, 0)
    own, ghost = call(fold_body, [tile, tile], [VMEM] * 4, flops=1000000000)(accum, above, below, pack)
    below, above = shifted(ghost, "gx")
    forces, following = call(
        last_body, [shape(*coords.shape), shape(*cheb_cur.shape)], [VMEM] * 4, flops=200_000_000
    )(own, above, below, tail)
    return forces, following, call(moments_body, shape(2, 4), [VMEM])(shares)


def solution(mesh):
    return jax.shard_map(
        local,
        mesh=mesh,
        in_specs=(
            P(None, "gx", "gy", None),
            P("gx", "gy", None),
            P("gx", "gy", None, None),
            P("gx", "gy", None, None),
            P("gx", "gy", None, None),
            P(),
            P(),
            P(),
            P(),
            P(),
            P(),
            P(None, None, "gx", "gy", None),
            P(None, None, "gx", "gy", None),
        ),
        out_specs=(P(None, "gx", "gy", None), P(None, None, "gx", "gy", None), P()),
        check_vma=False,
    )
```
